256 devices in a mesh: seq: 8 (over y, core), exp: 32 (over z, x).
Axes of the slice: x: 4, y: 4, z: 8, core: 2. Of those that a mesh axis runs over, the one named last changes fastest.
Arguments:
- queries: bfloat16 [2048, 64, 576], P('seq', 'exp')
- latent_cache: bfloat16 [32, 64, 576], P('seq')
- ancestors: int32 [32, 8], P('seq'), may hold values from -1 to 31, as said below
- value_up: bfloat16 [64, 512, 128], P('exp'), may hold values from -1 to 1
- out_proj: bfloat16 [8192, 7168], P('exp'), may hold values from -0.0625 to 0.0625
- residual: bfloat16 [2048, 7168], P(('seq', 'exp')), may hold values from -6 to 6
- norm_gain: bfloat16 [7168], replicated, may hold values from 0.099609375 to 1.8984375
- routes: int32 [2048, 8], P(('seq', 'exp')), may hold values from 0 to 31, all different within a row; in each aligned block of 8 rows (0 to 7, 8 to 15, ...) at most 3 rows name the same one
- gates: float32 [2048, 8], P(('seq', 'exp')), may hold values from 0.05 to 0.6
- w_gate: bfloat16 [32, 7168, 1024], P('exp', None, 'seq'), may hold values from -0.0625 to 0.0625
- w_up: bfloat16 [32, 7168, 1024], P('exp', None, 'seq'), may hold values from -0.0625 to 0.0625
- w_down: bfloat16 [32, 1024, 7168], P('exp', 'seq'), may hold values from -0.1875 to 0.1875
Outputs:
- layer_out: bfloat16 [2048, 7168], P(('seq', 'exp'))
The draws below stay inside these ranges and needn't reach their ends.
Inputs may be any that keep to these rules, and one draw needn't show every extreme that they name: `ancestors`: each row lists distinct segments other than its own, listed ones first and then -1; every row lists at least one, some row lists 8 and some row exactly one. `routes`: within the 8 rows of one device no expert is named more than 3 times, a bound that some block reaches there.
All inputs are finite; a program needn't handle non-finite values.
Results may differ from the reference program's by a relative error of at most 0.024.
Values may be sent and summed in bfloat16 or wider, within the bound.
A program may use at most 128 MiB of HBM per device.

```python
import math
import jax
import jax.numpy as jnp
import numpy as np
from jax import lax

D = 7168
LAT = 512
ROPE = 64
HD = 128
HEADS = 64
FF_DEV = 128
EFF = 1024
EXPERTS = 32
TOP = 8
BLK = 64
TOK_DEV = 8
SEGMENTS = 32
TOKENS = 2048
ANC = 8
CAP = 3
N_SEQ = 8


def shared_latent(key):
    return jax.random.normal(key, (SEGMENTS, BLK, LAT + ROPE), jnp.float32)


def draw_latent_cache(key, part):
    base = shared_latent(key)
    return base.astype(jnp.bfloat16)


def draw_queries(key, part):
    key = jax.random.fold_in(key, 11)
    first = jax.random.fold_in(key, 0)
    shape = (TOKENS, HEADS, LAT + ROPE)
    values = 0.6 * jax.random.normal(first, shape, jnp.float32)
    return values.astype(jnp.bfloat16)


def draw_ancestors(key, part):
    key = jax.random.fold_in(key, 23)
    first, second = jax.random.split(key)
    order_scores = jax.random.randint(first, (SEGMENTS, SEGMENTS - 1), 0, 2 ** 20) * SEGMENTS
    order_scores = order_scores + jnp.arange(SEGMENTS - 1, dtype=jnp.int32)[None, :]
    offsets = jnp.argsort(order_scores, axis=1)[:, :ANC].astype(jnp.int32) + 1
    listed = (jnp.arange(SEGMENTS, dtype=jnp.int32)[:, None] + offsets) % SEGMENTS
    counts = jax.random.randint(second, (SEGMENTS,), 1, ANC + 1)
    counts = counts.at[0].set(ANC).at[1].set(1)
    return jnp.where(jnp.arange(ANC, dtype=jnp.int32)[None, :] < counts[:, None], listed, -1).astype(jnp.int32)


def levels(key, extent, pieces, smallest, largest):
    def one(axis_at, shards_of):
        draws = jax.random.uniform(jax.random.fold_in(jax.random.fold_in(key, 6), axis_at), (shards_of,), jnp.float32, smallest / len(pieces), largest / len(pieces))
        return jnp.repeat(jnp.exp(draws), extent[axis_at] // shards_of).reshape((-1,) + (1,) * (len(extent) - axis_at - 1))

    gain = one(*pieces[0])
    for cut in pieces[1:]:
        gain = gain * one(*cut)
    return gain


def deal_out(stream_key, own, number, rows, count, top, limit, lean):
    order = jax.random.permutation(stream_key, count)
    heavy_load, common = shares(count, rows * top, limit, lean, True), shares(count, rows * top, limit, lean, False)
    places = jnp.arange(count)

    def named(sizes, turn):
        used = int((sizes > 0).sum())
        fixed = max(1, used // 4)
        moved = fixed + (places - fixed + turn * (used - fixed)) % max(1, count - fixed)
        return jnp.zeros((count,), jnp.int32).at[order[jnp.where(places < fixed, places, moved)]].set(jnp.asarray(sizes, jnp.int32))

    sizes = jnp.where(number % 4 == 0, named(heavy_load, number // 4), named(common, number - number // 4 - 1))
    mixed = jax.random.permutation(jax.random.fold_in(own, 3), count)
    giver, receiver = mixed[0:count // 2 * 2:2], mixed[1:count // 2 * 2:2]
    slack = jnp.minimum(sizes[giver] - 1, limit - sizes[receiver]) // 2
    slack = jnp.where((giver == order[0]) | (receiver == order[0]) | (sizes[receiver] == 0), 0, jnp.maximum(slack, 0))
    moved = jax.random.randint(jax.random.fold_in(own, 4), (count // 2,), 0, 1 << 20) % (slack + 1)
    sizes = sizes.at[giver].add(-moved).at[receiver].add(moved)
    labels = jnp.searchsorted(jnp.cumsum(sizes), jnp.arange(rows * top), side="right").astype(jnp.int32)
    grid = labels.reshape(top, rows).T
    grid = grid[jax.random.permutation(jax.random.fold_in(own, 1), rows)]
    turn = jax.random.randint(jax.random.fold_in(own, 2), (rows, 1), 0, top)
    return jnp.take_along_axis(grid, (jnp.arange(top)[None, :] + turn) % top, axis=1)


def shares(number_of, total, bound, lean, full):
    portions = [(1 << 20) // math.isqrt(rank ** lean) + 1 for rank in range(1, number_of + 1)]
    largest = bound if full else min(bound, max(-(-total // number_of), total * portions[0] // sum(portions)))
    least = 1 if total - largest >= number_of - 1 else 0
    holding, spare = [largest] + [least] * (number_of - 1), total - largest - least * (number_of - 1)
    while spare > 0:
        candidates = [i for i in range(1, number_of) if holding[i] < largest] or [i for i in range(1, number_of) if holding[i] < bound]
        pool, remaining = sum([portions[i] for i in candidates]), spare
        for i in candidates:
            addition = min(bound - holding[i], max(1, remaining * portions[i] // pool), spare)
            holding[i] = holding[i] + addition
            spare = spare - addition
    return np.array(holding)


def scatter_about(own_key, dims, spread, reach, cuts=(), kind=jnp.bfloat16):
    factor_of = levels(own_key, dims, cuts, -0.22, 0.18) if cuts else 1.0
    entries = jax.random.normal(own_key, dims, jnp.float32) * spread * factor_of
    return jnp.minimum(jnp.maximum(entries, -reach), reach).astype(kind)


def setup_inputs(seed: int = 0) -> dict:
    seeds = jax.random.split(jax.random.key(seed), 13)
    queries = draw_queries(jax.random.fold_in(seeds[12], 71), 0)
    latent_cache = draw_latent_cache(jax.random.fold_in(seeds[12], 71), 0)
    ancestors = draw_ancestors(jax.random.fold_in(seeds[12], 71), 0)
    value_up = scatter_about(seeds[3], (HEADS, LAT, HD), (LAT // 16) ** -0.5, 1.0, ((0, 32),))
    out_proj = scatter_about(seeds[4], (HEADS * HD, D), (HEADS * HD) ** -0.5, 0.0625, ((0, 32),))
    residual = scatter_about(seeds[5], (TOKENS, D), 0.5, 6.0, ((0, 256),))
    norm_gain = jnp.clip(1.0 + 0.18 * jax.random.normal(seeds[6], (D,), jnp.float32), 0.099609375, 1.8984375).astype(jnp.bfloat16)
    routes_keys = jax.random.split(jax.random.fold_in(seeds[7], 1), TOKENS // TOK_DEV)
    routes_turns = jax.random.permutation(jax.random.fold_in(seeds[7], 3), TOKENS // TOK_DEV)
    routes = jax.vmap(lambda own, number: deal_out(jax.random.fold_in(seeds[7], 2), own, number, TOK_DEV, EXPERTS, TOP, CAP, 2))(routes_keys, routes_turns).reshape((TOKENS, TOP))
    gates = jnp.clip(jnp.exp(math.log(0.6) - 2.4849067 * jax.random.uniform(seeds[8], (TOKENS, TOP), jnp.float32) ** levels(seeds[8], (TOKENS, TOP), ((0, 256),), -0.2, 0.2)), 0.05, 0.6)
    w_gate = scatter_about(seeds[9], (EXPERTS, D, EFF), D ** -0.5, 0.0625, ((0, 32), (2, 8)))
    w_up = scatter_about(seeds[10], (EXPERTS, D, EFF), D ** -0.5, 0.0625, ((0, 32), (2, 8)))
    w_down = scatter_about(seeds[11], (EXPERTS, EFF, D), EFF ** -0.5, 0.1875, ((0, 32), (1, 8)))
    return dict(queries=queries, latent_cache=latent_cache, ancestors=ancestors, value_up=value_up, out_proj=out_proj, residual=residual, norm_gain=norm_gain, routes=routes, gates=gates, w_gate=w_gate, w_up=w_up, w_down=w_down)


neg_large = -1e+30
eps_norm = 1e-06

def slot_positions(block_routes, experts, capacity):
    flat = block_routes.reshape(-1)
    onehot = (flat[:, None] == jnp.arange(experts, dtype=jnp.int32)[None, :]).astype(jnp.int32)
    before = jnp.cumsum(onehot, axis=0) - onehot
    slots = lax.optimization_barrier(jnp.sum(before * onehot, axis=1))
    return (flat * capacity + slots).reshape(block_routes.shape).astype(jnp.int32)

def reference(queries, latent_cache, ancestors, value_up, out_proj, residual, norm_gain, routes, gates, w_gate, w_up, w_down):
    scale = (HD + ROPE) ** (-0.5)
    width = LAT + ROPE
    causal = jnp.arange(BLK)[:, None] >= jnp.arange(BLK)[None, :]
    query_blocks = queries.reshape(SEGMENTS, BLK, HEADS, width)

    def one_segment(index):
        query = query_blocks[index].astype(jnp.float32)
        listed = ancestors[index]
        live = listed >= 0
        picked = latent_cache[jnp.maximum(listed, 0)].reshape(ANC * BLK, width)
        keys = jnp.concatenate([picked, latent_cache[index]], axis=0).astype(jnp.float32)
        far_mask = jnp.broadcast_to(jnp.repeat(live, BLK)[None, :], (BLK, ANC * BLK))
        mask = jnp.concatenate([far_mask, causal], axis=1)[:, None, :]
        scores = jnp.einsum('qhc,kc->qhk', query, keys) * scale
        highest = lax.optimization_barrier(jnp.max(jnp.where(mask, scores, neg_large), axis=-1, keepdims=True))
        weights = jnp.where(mask, jnp.exp(scores - highest), 0.0)
        total = lax.optimization_barrier(jnp.sum(weights, axis=-1))
        probs = weights.astype(jnp.bfloat16).astype(jnp.float32)
        summed = jnp.einsum('qhk,kc->qhc', probs, keys[:, :LAT])
        return (summed / total[:, :, None]).astype(jnp.bfloat16)
    latent_out = lax.map(one_segment, jnp.arange(SEGMENTS, dtype=jnp.int32)).reshape(TOKENS, HEADS, LAT)
    head_out = jnp.einsum('thc,hcv->thv', latent_out.astype(jnp.float32), value_up.astype(jnp.float32))
    head_out = head_out.astype(jnp.bfloat16).reshape(TOKENS, HEADS * HD)
    attention = jnp.dot(head_out, out_proj, preferred_element_type=jnp.float32)
    hidden_state = residual.astype(jnp.float32) + attention
    inverse = lax.rsqrt(lax.optimization_barrier(jnp.mean(hidden_state * hidden_state, axis=1, keepdims=True)) + eps_norm)
    normed = (hidden_state * inverse * norm_gain.astype(jnp.float32)).astype(jnp.bfloat16)
    blocks = TOKENS // TOK_DEV
    block_routes = routes.reshape(blocks, TOK_DEV, TOP)
    positions = jax.vmap(lambda rows: slot_positions(rows, EXPERTS, CAP))(block_routes)
    block_ids = jnp.broadcast_to(jnp.arange(blocks, dtype=jnp.int32)[:, None, None], positions.shape)
    token_ids = block_ids * TOK_DEV + jnp.broadcast_to(jnp.arange(TOK_DEV, dtype=jnp.int32)[None, :, None], positions.shape)
    table = jnp.full((blocks, EXPERTS * CAP), -1, jnp.int32)
    table = table.at[block_ids, positions].set(token_ids)
    table = table.reshape(blocks, EXPERTS, CAP).transpose(1, 0, 2).reshape(EXPERTS, blocks * CAP)

    def one_expert(index):
        ids = table[index]
        rows = jnp.where((ids >= 0)[:, None], normed[jnp.maximum(ids, 0)], jnp.zeros((), jnp.bfloat16))
        gate_val = jnp.dot(rows, w_gate[index], preferred_element_type=jnp.float32)
        up_val = jnp.dot(rows, w_up[index], preferred_element_type=jnp.float32)
        act = (jax.nn.silu(gate_val) * up_val).astype(jnp.bfloat16)
        down = w_down[index].reshape(N_SEQ, FF_DEV, D).astype(jnp.float32)
        grouped = act.reshape(blocks * CAP, N_SEQ, FF_DEV).astype(jnp.float32)
        parts = jnp.einsum('rsf,sfd->srd', grouped, down).astype(jnp.bfloat16)
        parts = lax.optimization_barrier(parts).astype(jnp.float32)
        return lax.optimization_barrier(jnp.sum(parts, axis=0)).astype(jnp.bfloat16)
    expert_out = lax.map(one_expert, jnp.arange(EXPERTS, dtype=jnp.int32))
    flat_out = expert_out.reshape(EXPERTS * blocks * CAP, D)
    slots = positions - block_routes * CAP
    flat_index = block_routes * (blocks * CAP) + block_ids * CAP + slots
    picked = flat_out[flat_index.reshape(-1)].reshape(TOKENS, TOP, D).astype(jnp.float32)
    moe = lax.optimization_barrier(jnp.sum(gates[:, :, None] * picked, axis=1))
    return (hidden_state + moe).astype(jnp.bfloat16)
```

```python
import jax
import jax.numpy as jnp
from jax import lax
from jax.experimental import pallas as pl
from jax.experimental.pallas import tpu as pltpu
from jax.sharding import PartitionSpec as P

D = 7168
LAT = 512
ROPE = 64
HD = 128
BLK = 64
ANC = 8
TOP = 8
EXPERTS = 32
CAP = 3
NY, NZ, NX = 4, 8, 4
DY = D // NY
CW = 512
FF = 1024
NORM_EPS = 1e-6
MASKED = -1e30
F32 = jnp.float32
BF16 = jnp.bfloat16
ANY = pl.BlockSpec(memory_space=pl.ANY)
VMEM = pl.BlockSpec(memory_space=pltpu.VMEM)
SMEM = pl.BlockSpec(memory_space=pltpu.SMEM)
DMA = pltpu.SemaphoreType.DMA


def place():
    s = lax.axis_index("seq")
    e = lax.axis_index("exp")
    return lax.div(s, 2), lax.rem(s, 2), lax.div(e, NX), lax.rem(e, NX)


def wrap(value, count):
    return lax.rem(value + count, count)


def remote(src, dst, send_sem, recv_sem, y, c, z, x):
    return pltpu.make_async_remote_copy(
        src_ref=src,
        dst_ref=dst,
        send_sem=send_sem,
        recv_sem=recv_sem,
        device_id=(y * 2 + c, z * NX + x),
        device_id_type=pl.DeviceIdType.MESH,
    )


def meet(peers):
    barrier = pltpu.get_barrier_semaphore()
    for y, c, z, x in peers:
        pl.semaphore_signal(
            barrier,
            inc=1,
            device_id=(y * 2 + c, z * NX + x),
            device_id_type=pl.DeviceIdType.MESH,
        )
    pl.semaphore_wait(barrier, len(peers))


def y_peers(y, c, z, x):
    return [(wrap(y + d, NY), c, z, x) for d in range(1, NY)]


def z_peers(y, c, z, x):
    return [(y, c, wrap(z + d, NZ), x) for d in range(1, NZ)]


def x_peers(y, c, z, x):
    return [(y, c, z, wrap(x + d, NX)) for d in range(1, NX)]


def column_start(x):
    return jnp.minimum(x * CW, DY - CW)


def pre_kernel(
    lat, outp, meta, res, lat_all, op_all, meta_all, res_y,
    loc, lat_s, lat_r, fwd_s, fwd_r, op_s, op_r, me_s, me_r, mz_s, mz_r, re_s, re_r,
):
    y, c, z, x = place()
    s = y * 2 + c
    other = 1 - c
    meet(
        y_peers(y, c, z, x) + z_peers(y, c, z, x) + x_peers(y, c, z, x) + [(y, other, z, x)]
    )
    started = []

    def go(copy):
        copy.start()
        started.append(copy)

    for d in range(1, NY):
        go(remote(lat, lat_all.at[s], lat_s.at[d], lat_r.at[d], wrap(y + d, NY), c, z, x))
    go(remote(lat, lat_all.at[s], fwd_s.at[0], fwd_r.at[0], y, other, z, x))

    def columns(to):
        start = pl.multiple_of(y * DY + column_start(to), 128)
        return outp.at[:, pl.ds(start, CW)]

    for d in range(1, NY):
        to = wrap(y + d, NY)
        go(remote(meta, meta_all.at[z, y], me_s.at[d], me_r.at[d], to, c, z, x))
        part = res.at[:, pl.ds(pl.multiple_of(to * DY, 128), DY)]
        go(remote(part, res_y.at[y], re_s.at[d], re_r.at[d], to, c, z, x))
    for d in range(1, NX):
        to = wrap(x + d, NX)
        go(remote(columns(to), op_all.at[x], op_s.at[d], op_r.at[d], y, c, z, to))
    own = [
        pltpu.make_async_copy(meta, meta_all.at[z, y], loc.at[0]),
        pltpu.make_async_copy(lat, lat_all.at[s], loc.at[1]),
        pltpu.make_async_copy(columns(x), op_all.at[x], loc.at[2]),
        pltpu.make_async_copy(
            res.at[:, pl.ds(pl.multiple_of(y * DY, 128), DY)], res_y.at[y], loc.at[3]
        ),
    ]
    for copy in own:
        copy.start()

    own[0].wait()
    for d in range(1, NY):
        src = wrap(y - d, NY)
        remote(meta, meta_all.at[z, src], me_s.at[d], me_r.at[d], y, c, z, x).wait_recv()
    for d in range(1, NZ):
        go(remote(meta_all.at[z], meta_all.at[z], mz_s.at[d], mz_r.at[d], y, c, wrap(z + d, NZ), x))
    for d in (1, 3, 2):
        block = lat_all.at[wrap(y - d, NY) * 2 + c]
        remote(lat, block, lat_s.at[d], lat_r.at[d], y, c, z, x).wait_recv()
        go(remote(block, block, fwd_s.at[d], fwd_r.at[d], y, other, z, x))
    for d in range(NY):
        block = lat_all.at[wrap(y - d, NY) * 2 + other]
        remote(lat, block, fwd_s.at[d], fwd_r.at[d], y, c, z, x).wait_recv()
    for d in range(1, NZ):
        src = meta_all.at[wrap(z - d, NZ)]
        remote(src, src, mz_s.at[d], mz_r.at[d], y, c, z, x).wait_recv()
    for d in range(1, NX):
        src = op_all.at[wrap(x - d, NX)]
        remote(src, src, op_s.at[d], op_r.at[d], y, c, z, x).wait_recv()
    for d in range(1, NY):
        src = res_y.at[wrap(y - d, NY)]
        remote(src, src, re_s.at[d], re_r.at[d], y, c, z, x).wait_recv()
    for copy in own[1:]:
        copy.wait()
    for copy in started:
        copy.wait_send()


def exchange_first(lat, outp, meta, res):
    return pl.pallas_call(
        pre_kernel,
        out_shape=(
            jax.ShapeDtypeStruct((8,) + lat.shape, BF16),
            jax.ShapeDtypeStruct((NX, 256, CW), BF16),
            jax.ShapeDtypeStruct((NZ, NY, 8, 128), F32),
            jax.ShapeDtypeStruct((NY, 8, DY), F32),
        ),
        in_specs=[ANY] * 4,
        out_specs=(ANY,) * 4,
        scratch_shapes=[
            DMA((4,)),
            DMA((NY,)), DMA((NY,)),
            DMA((NY,)), DMA((NY,)),
            DMA((NX,)), DMA((NX,)),
            DMA((NY,)), DMA((NY,)),
            DMA((NZ,)), DMA((NZ,)),
            DMA((NY,)), DMA((NY,)),
        ],
        compiler_params=pltpu.CompilerParams(collective_id=0, has_side_effects=True),
        name="exchange_first",
    )(lat, outp, meta, res)


def attend_kernel(anc, q, lat_all, live, vup, out, keys):
    s = lax.axis_index("seq")
    scale = (HD + ROPE) ** (-0.5)
    width = (ANC + 1) * BLK
    col = lax.broadcasted_iota(jnp.int32, (2 * BLK, width), 1)
    row = lax.rem(lax.broadcasted_iota(jnp.int32, (2 * BLK, width), 0), BLK)
    near = row >= col - ANC * BLK
    for g in range(4):
        for a in range(ANC):
            keys[a * BLK : (a + 1) * BLK, :] = lat_all[jnp.maximum(anc[g, a], 0)]
        keys[ANC * BLK :, :] = lat_all[s * 4 + g]
        query = q[:, g * BLK : (g + 1) * BLK, :].reshape(2 * BLK, LAT + ROPE)
        scores = (
            lax.dot_general(
                query, keys[...], (((1,), (1,)), ((), ())), preferred_element_type=F32
            )
            * scale
        )
        mask = jnp.logical_and(near, live[g : g + 1, :] > 0.5)
        highest = jnp.max(jnp.where(mask, scores, MASKED), axis=1, keepdims=True)
        weights = jnp.where(mask, jnp.exp(scores - highest), 0.0)
        total = jnp.sum(weights, axis=1, keepdims=True)
        summed = jnp.dot(weights.astype(BF16), keys[:, :LAT], preferred_element_type=F32)
        latent = (summed / total).astype(BF16)
        for h in range(2):
            value = jnp.dot(
                latent[h * BLK : (h + 1) * BLK], vup[h], preferred_element_type=F32
            )
            out[g * BLK : (g + 1) * BLK, h * HD : (h + 1) * HD] = value.astype(BF16)


def attend(anc, q, lat_all, live, vup):
    return pl.pallas_call(
        attend_kernel,
        out_shape=jax.ShapeDtypeStruct((256, 256), BF16),
        in_specs=[SMEM, VMEM, VMEM, VMEM, VMEM],
        out_specs=VMEM,
        scratch_shapes=[pltpu.VMEM(((ANC + 1) * BLK, LAT + ROPE), BF16)],
        compiler_params=pltpu.CompilerParams(vmem_limit_bytes=24 << 20),
        name="attend",
    )(anc, q, lat_all, live, vup)


def mid_kernel(
    ho, op_all, res_y, gain, choose, wg, wu, wd,
    hidden, rows, wg_all, wu_all, wd_all,
    ho_all, zsend, zrecv, att, xrecv, squares, tokens, disp,
    loc, ho_s, ho_r, zs, zr, xs, xr, qs, qr, ts, tr, ds, dr, w_s, w_r, f_s, f_r,
):
    y, c, z, x = place()
    s = y * 2 + c
    other = 1 - c
    corners = [
        (dy, dx) for dy in range(NY) for dx in range(NX) if (dy, dx) != (0, 0)
    ]
    meet(
        [(wrap(y + dy, NY), c, z, wrap(x + dx, NX)) for dy, dx in corners]
        + z_peers(y, c, z, x)
        + [(y, other, z, x)]
    )
    started = []

    def go(copy):
        copy.start()
        started.append(copy)

    for dy, dx in corners:
        i = dy * NX + dx
        go(
            remote(
                ho, ho_all.at[y, x], ho_s.at[i], ho_r.at[i],
                wrap(y + dy, NY), c, z, wrap(x + dx, NX),
            )
        )
    ho_all[y, x] = ho[...]

    def weight_parts(to):
        at = pl.ds(pl.multiple_of(to * DY, 128), DY)
        return (
            (wg.at[at, :], wg_all, 0),
            (wu.at[at, :], wu_all, 1),
            (wd.at[:, at], wd_all, 2),
        )

    own = []
    for src, dst, k in weight_parts(y):
        own.append(pltpu.make_async_copy(src, dst.at[s], loc.at[k]))
        go(remote(src, dst.at[s], f_s.at[k, 0], f_r.at[k, 0], y, other, z, x))
    for copy in own:
        copy.start()

    for dy in range(NY):
        ys = wrap(y - dy, NY)
        total = None
        for dx in range(NX):
            xn = wrap(x - dx, NX)
            i = dy * NX + dx
            if i:
                remote(ho, ho_all.at[ys, xn], ho_s.at[i], ho_r.at[i], y, c, z, x).wait_recv()
            part = jnp.dot(ho_all[ys, xn], op_all[xn], preferred_element_type=F32)
            total = part if total is None else total + part
        total = total.astype(BF16)
        for k in range(NZ):
            zsend[k, ys] = total[k * 32 : (k + 1) * 32]
        for d in range(1, NZ):
            to = wrap(z + d, NZ)
            go(
                remote(
                    zsend.at[to, ys], zrecv.at[d, ys], zs.at[d, dy], zr.at[d, dy], y, c, to, x
                )
            )
    for d in (1, 3, 2):
        to = wrap(y + d, NY)
        for src, dst, k in weight_parts(to):
            go(remote(src, dst.at[s], w_s.at[k, d], w_r.at[k, d], to, c, z, x))

    for dy in range(NY):
        ys = wrap(y - dy, NY)
        total = zsend[z, ys].astype(F32)
        for d in range(1, NZ):
            part = zrecv.at[d, ys]
            remote(part, part, zs.at[d, dy], zr.at[d, dy], y, c, z, x).wait_recv()
            total = total + zrecv[d, ys].astype(F32)
        for k in range(NX):
            att[k, ys] = total[k * 8 : (k + 1) * 8]
    for d in range(1, NX):
        to = wrap(x + d, NX)
        go(remote(att.at[to], xrecv.at[x], xs.at[d], xr.at[d], y, c, z, to))
    xrecv[x] = att[x]
    for d in range(1, NX):
        part = xrecv.at[wrap(x - d, NX)]
        remote(part, part, xs.at[d], xr.at[d], y, c, z, x).wait_recv()
    for k in range(NX):
        low = 256 if k == NX - 1 else 0
        at = k * CW
        wide = CW - low
        hidden[:, at : at + wide] = (
            xrecv[k].reshape(NY * 8, CW)[:, low:]
            + res_y[:, :, at : at + wide].reshape(NY * 8, wide)
        )
    held = hidden[...]
    squares[y] = jnp.broadcast_to(jnp.sum(held * held, axis=1, keepdims=True), (NY * 8, 128))
    for d in range(1, NY):
        go(remote(squares.at[y], squares.at[y], qs.at[d], qr.at[d], wrap(y + d, NY), c, z, x))
    for d in range(1, NY):
        part = squares.at[wrap(y - d, NY)]
        remote(part, part, qs.at[d], qr.at[d], y, c, z, x).wait_recv()
    mean = (squares[0] + squares[1] + squares[2] + squares[3])[:, :1] * (1.0 / D)
    tokens[z] = (held * lax.rsqrt(mean + NORM_EPS) * gain[...]).astype(BF16)
    for d in (4, 3, 5, 2, 6, 1, 7):
        go(remote(tokens.at[z], tokens.at[z], ts.at[d], tr.at[d], y, c, wrap(z + d, NZ), x))
    for d in range(1, NZ):
        part = tokens.at[wrap(z - d, NZ)]
        remote(part, part, ts.at[d], tr.at[d], y, c, z, x).wait_recv()
    table = tokens[...].reshape(NZ * 32, DY)
    for d in (2, 1, 3, 0):
        to = wrap(x + d, NX)
        disp[to] = jnp.dot(choose[to], table, preferred_element_type=F32).astype(BF16)
        if d:
            go(remote(disp.at[to], rows.at[x], ds.at[d], dr.at[d], y, c, z, to))
        else:
            last = pltpu.make_async_copy(disp.at[to], rows.at[x], loc.at[3])
            last.start()
            own.append(last)

    for d in (1, 3, 2):
        src = wrap(y - d, NY) * 2 + c
        for k, dst in enumerate((wg_all, wu_all, wd_all)):
            part = dst.at[src]
            remote(part, part, w_s.at[k, d], w_r.at[k, d], y, c, z, x).wait_recv()
            go(remote(part, part, f_s.at[k, d], f_r.at[k, d], y, other, z, x))
    for d in range(1, NX):
        part = rows.at[wrap(x - d, NX)]
        remote(part, part, ds.at[d], dr.at[d], y, c, z, x).wait_recv()
    for d in range(NY):
        src = wrap(y - d, NY) * 2 + other
        for k, dst in enumerate((wg_all, wu_all, wd_all)):
            part = dst.at[src]
            remote(part, part, f_s.at[k, d], f_r.at[k, d], y, c, z, x).wait_recv()
    for copy in own:
        copy.wait()
    for copy in started:
        copy.wait_send()


def project_and_dispatch(ho, op_all, res_y, gain, choose, wg, wu, wd):
    return pl.pallas_call(
        mid_kernel,
        out_shape=(
            jax.ShapeDtypeStruct((NY * 8, DY), F32),
            jax.ShapeDtypeStruct((NX, 96, DY), BF16),
            jax.ShapeDtypeStruct((8, DY, 128), BF16),
            jax.ShapeDtypeStruct((8, DY, 128), BF16),
            jax.ShapeDtypeStruct((8, 128, DY), BF16),
        ),
        in_specs=[VMEM] * 5 + [ANY] * 3,
        out_specs=(VMEM, ANY, ANY, ANY, ANY),
        scratch_shapes=[
            pltpu.VMEM((NY, NX, 256, 256), BF16),
            pltpu.VMEM((NZ, NY, 32, CW), BF16),
            pltpu.VMEM((NZ, NY, 32, CW), BF16),
            pltpu.VMEM((NX, NY, 8, CW), F32),
            pltpu.VMEM((NX, NY, 8, CW), F32),
            pltpu.VMEM((NY, NY * 8, 128), F32),
            pltpu.VMEM((NZ, NY * 8, DY), BF16),
            pltpu.VMEM((NX, 96, DY), BF16),
            DMA((4,)),
            DMA((16,)), DMA((16,)),
            DMA((NZ, NY)), DMA((NZ, NY)),
            DMA((NX,)), DMA((NX,)),
            DMA((NY,)), DMA((NY,)),
            DMA((NZ,)), DMA((NZ,)),
            DMA((NX,)), DMA((NX,)),
            DMA((3, NY)), DMA((3, NY)),
            DMA((3, NY)), DMA((3, NY)),
        ],
        compiler_params=pltpu.CompilerParams(
            collective_id=1, has_side_effects=True, vmem_limit_bytes=40 << 20
        ),
        name="project_and_dispatch",
    )(ho, op_all, res_y, gain, choose, wg, wu, wd)


def expert_kernel(
    rows, combine, hidden, wg_all, wu_all, wd_all,
    out,
    w_in, w_out, gsend, grecv, act, dout, back, zsend, zrecv, fin, orecv,
    loc, gs, gr, as_, ar, bs, br, zs, zr, os_, or_,
):
    y, c, z, x = place()
    fetch = []
    for k in range(8):
        at = pl.ds(k * 128, 128)
        fetch.append(pltpu.make_async_copy(wg_all.at[k], w_in.at[:, at], loc.at[0, k]))
        fetch.append(
            pltpu.make_async_copy(wu_all.at[k], w_in.at[:, pl.ds(FF + k * 128, 128)], loc.at[1, k])
        )
    for k in range(8):
        fetch.append(pltpu.make_async_copy(wd_all.at[k], w_out.at[pl.ds(k * 128, 128), :], loc.at[2, k]))
    for copy in fetch:
        copy.start()
    meet(y_peers(y, c, z, x) + z_peers(y, c, z, x) + x_peers(y, c, z, x))
    started = []

    def go(copy):
        copy.start()
        started.append(copy)

    for copy in fetch:
        copy.wait()
    every = rows[...].reshape(NX * 96, DY)

    def inward(j, _):
        at = pl.ds(pl.multiple_of(j * 512, 512), 512)
        part = jnp.dot(every, w_in[:, at], preferred_element_type=F32).astype(BF16)
        for k in range(NX):
            gsend[k, :, at] = part[k * 96 : (k + 1) * 96]
        return 0

    lax.fori_loop(0, 2 * FF // 512, inward, 0)
    for d in (2, 1, 3):
        to = wrap(y + d, NY)
        go(remote(gsend.at[to], grecv.at[d], gs.at[d], gr.at[d], to, c, z, x))
    summed = gsend[y].astype(F32)
    for d in (1, 3, 2):
        part = grecv.at[d]
        remote(part, part, gs.at[d], gr.at[d], y, c, z, x).wait_recv()
        summed = summed + grecv[d].astype(F32)
    gate = summed[:, :FF]
    act[y] = (gate / (1.0 + jnp.exp(-gate)) * summed[:, FF:]).astype(BF16)
    for d in (2, 1, 3):
        go(remote(act.at[y], act.at[y], as_.at[d], ar.at[d], wrap(y + d, NY), c, z, x))
    for d in (1, 3, 2):
        part = act.at[wrap(y - d, NY)]
        remote(part, part, as_.at[d], ar.at[d], y, c, z, x).wait_recv()
    acts = act[...].reshape(NX * 96, FF)

    def outward(j, _):
        at = pl.ds(pl.multiple_of(j * 256, 256), 256)
        part = jnp.dot(acts, w_out[:, at], preferred_element_type=F32).astype(BF16)
        for k in range(NX):
            dout[k, :, at] = part[k * 96 : (k + 1) * 96]
        return 0

    lax.fori_loop(0, DY // 256, outward, 0)
    for d in (2, 1, 3):
        to = wrap(x + d, NX)
        go(remote(dout.at[to], back.at[x], bs.at[d], br.at[d], y, c, z, to))
    back[x] = dout[x]
    for d in (1, 3, 2):
        part = back.at[wrap(x - d, NX)]
        remote(part, part, bs.at[d], br.at[d], y, c, z, x).wait_recv()

    def gather(j, _):
        at = pl.ds(pl.multiple_of(j * 256, 256), 256)
        part = jnp.dot(
            combine[...], back[:, :, at].reshape(NX * 96, 256), preferred_element_type=F32
        ).astype(BF16)
        for k in range(NZ):
            zsend[k, :, at] = part[k * 32 : (k + 1) * 32]
        return 0

    lax.fori_loop(0, DY // 256, gather, 0)
    for d in (4, 3, 5, 2, 6, 1, 7):
        to = wrap(z + d, NZ)
        go(remote(zsend.at[to], zrecv.at[d], zs.at[d], zr.at[d], y, c, to, x))
    total = hidden[...] + zsend[z].astype(F32)
    for d in range(1, NZ):
        part = zrecv.at[d]
        remote(part, part, zs.at[d], zr.at[d], y, c, z, x).wait_recv()
        total = total + zrecv[d].astype(F32)
    for k in range(NY):
        fin[k] = total[k * 8 : (k + 1) * 8]
    for d in range(1, NY):
        to = wrap(y + d, NY)
        go(remote(fin.at[to], orecv.at[y], os_.at[d], or_.at[d], to, c, z, x))
    orecv[y] = fin[y]
    for d in range(1, NY):
        part = orecv.at[wrap(y - d, NY)]
        remote(part, part, os_.at[d], or_.at[d], y, c, z, x).wait_recv()
    for k in range(NY):
        out[:, k * DY : (k + 1) * DY] = orecv[k]
    for copy in started:
        copy.wait_send()


def run_experts(rows, combine, hidden, wg_all, wu_all, wd_all):
    return pl.pallas_call(
        expert_kernel,
        out_shape=jax.ShapeDtypeStruct((8, D), F32),
        in_specs=[VMEM] * 3 + [ANY] * 3,
        out_specs=VMEM,
        scratch_shapes=[
            pltpu.VMEM((DY, 2 * FF), BF16),
            pltpu.VMEM((FF, DY), BF16),
            pltpu.VMEM((NY, 96, 2 * FF), BF16),
            pltpu.VMEM((NY, 96, 2 * FF), BF16),
            pltpu.VMEM((NY, 96, FF), BF16),
            pltpu.VMEM((NX, 96, DY), BF16),
            pltpu.VMEM((NX, 96, DY), BF16),
            pltpu.VMEM((NZ, NY * 8, DY), BF16),
            pltpu.VMEM((NZ, NY * 8, DY), BF16),
            pltpu.VMEM((NY, 8, DY), F32),
            pltpu.VMEM((NY, 8, DY), F32),
            DMA((3, 8)),
            DMA((NY,)), DMA((NY,)),
            DMA((NY,)), DMA((NY,)),
            DMA((NX,)), DMA((NX,)),
            DMA((NZ,)), DMA((NZ,)),
            DMA((NY,)), DMA((NY,)),
        ],
        compiler_params=pltpu.CompilerParams(
            collective_id=2, has_side_effects=True, vmem_limit_bytes=48 << 20
        ),
        name="run_experts",
    )(rows, combine, hidden, wg_all, wu_all, wd_all)


def on_device(
    queries,
    latent_cache,
    ancestors,
    value_up,
    out_proj,
    residual,
    norm_gain,
    routes,
    gates,
    w_gate,
    w_up,
    w_down,
):
    y, c, z, x = place()
    flat = routes.reshape(-1)
    earlier = jnp.arange(64)[:, None] > jnp.arange(64)[None, :]
    slots = jnp.sum(
        jnp.logical_and(earlier, flat[:, None] == flat[None, :]).astype(jnp.int32), axis=1
    )
    positions = (flat * CAP + slots).reshape(8, TOP).astype(F32)
    meta = jnp.concatenate([positions, gates, jnp.zeros((8, 128 - 2 * TOP), F32)], axis=1)
    lat_all, op_all, meta_all, res_y = exchange_first(
        latent_cache, out_proj, meta, residual.astype(F32)
    )
    live = jnp.concatenate(
        [jnp.repeat((ancestors >= 0).astype(F32), BLK, axis=1), jnp.ones((4, BLK), F32)], axis=1
    )
    head_out = attend(
        ancestors,
        queries.transpose(1, 0, 2),
        lat_all.reshape(32, BLK, LAT + ROPE),
        live,
        value_up,
    )
    table = meta_all.reshape(256, 128)
    where = table[:, :TOP].astype(jnp.int32)
    row = jnp.arange(384, dtype=jnp.int32)
    wanted = (z * NX + row // 96) * CAP + row % CAP
    block = (row % 96) // CAP
    same = block[:, None] == (jnp.arange(256, dtype=jnp.int32) // 8)[None, :]
    hit = jnp.logical_and(where.T[None, :, :] == wanted[:, None, None], same[:, None, :])
    choose = jnp.any(hit, axis=1).astype(BF16).reshape(NX, 96, 256)
    hit_t = jnp.logical_and(where[:, :, None] == wanted[None, None, :], same.T[:, None, :])
    combine = jnp.sum(jnp.where(hit_t, table[:, TOP : 2 * TOP, None], 0.0), axis=1).astype(BF16)
    gain = lax.dynamic_slice(norm_gain, (y * DY,), (DY,)).astype(F32).reshape(1, DY)
    hidden, rows, wg_all, wu_all, wd_all = project_and_dispatch(
        head_out, op_all, res_y, gain, choose, w_gate[0], w_up[0], w_down[0]
    )
    final = run_experts(rows, combine, hidden, wg_all, wu_all, wd_all)
    return final.astype(BF16)


def solution(mesh):
    placed = (
        P("seq", "exp", None),
        P("seq", None, None),
        P("seq", None),
        P("exp", None, None),
        P("exp", None),
        P(("seq", "exp"), None),
        P(),
        P(("seq", "exp"), None),
        P(("seq", "exp"), None),
        P("exp", None, "seq"),
        P("exp", None, "seq"),
        P("exp", "seq", None),
    )
    return jax.shard_map(
        on_device, mesh=mesh, in_specs=placed, out_specs=P(("seq", "exp"), None), check_vma=False
    )
```

```python
import jax
import jax.numpy as jnp
from jax import lax
from jax.experimental import pallas as pl
from jax.experimental.pallas import tpu as pltpu
from jax.sharding import PartitionSpec as P

D = 7168
LAT = 512
ROPE = 64
HD = 128
BLK = 64
ANC = 8
TOP = 8
CAP = 3
NY, NZ, NX = 4, 8, 4
DY = D // NY
CW = 512
FF = 1024
HALF = 48
UNNAMED = 99.0
NORM_EPS = 1e-6
MASKED = -1e30
F32 = jnp.float32
BF16 = jnp.bfloat16
ANY = pl.BlockSpec(memory_space=pl.ANY)
VMEM = pl.BlockSpec(memory_space=pltpu.VMEM)
SMEM = pl.BlockSpec(memory_space=pltpu.SMEM)
DMA = pltpu.SemaphoreType.DMA


def place():
    s = lax.axis_index("seq")
    e = lax.axis_index("exp")
    return lax.div(s, 2), lax.rem(s, 2), lax.div(e, NX), lax.rem(e, NX)


def wrap(value, count):
    return lax.rem(value + count, count)


def meet(peers):
    barrier = pltpu.get_barrier_semaphore()
    for y, c, z, x in peers:
        pl.semaphore_signal(
            barrier,
            inc=1,
            device_id=(y * 2 + c, z * NX + x),
            device_id_type=pl.DeviceIdType.MESH,
        )
    pl.semaphore_wait(barrier, len(peers))


class Links:
    def __init__(self, y, c, z, x):
        self.at = (y, c, z, x)
        self.started = []

    def copy(self, src, dst, send_sem, recv_sem, y=None, c=None, z=None, x=None):
        here = self.at
        y, c, z, x = (own if new is None else new for new, own in zip((y, c, z, x), here))
        return pltpu.make_async_remote_copy(
            src_ref=src,
            dst_ref=dst,
            send_sem=send_sem,
            recv_sem=recv_sem,
            device_id=(y * 2 + c, z * NX + x),
            device_id_type=pl.DeviceIdType.MESH,
        )

    def send(self, src, dst, send_sem, recv_sem, **to):
        copy = self.copy(src, dst, send_sem, recv_sem, **to)
        copy.start()
        self.started.append(copy)

    def arrived(self, dst, send_sem, recv_sem):
        self.copy(dst, dst, send_sem, recv_sem).wait_recv()

    def finish(self):
        for copy in self.started:
            copy.wait_send()


def ring_gather(links, axis, count, me, view, half, send_sem, recv_sem):
    last = count // 2
    for step in range(1, last + 1):
        new = []
        for way, sign in enumerate((1, -1)):
            k = -sign * (step - 1)
            if step > 1:
                links.arrived(view(k, 0), send_sem.at[way, step - 1], recv_sem.at[way, step - 1])
                new.append(k)
            src, dst = view(k, 0), view(k, sign)
            if step == last:
                src, dst = half(src, way), half(dst, way)
            links.send(
                src, dst, send_sem.at[way, step], recv_sem.at[way, step],
                **{axis: wrap(me + sign, count)},
            )
        if new:
            yield new
    for way, sign in enumerate((1, -1)):
        links.arrived(
            half(view(-sign * last, 0), way), send_sem.at[way, last], recv_sem.at[way, last]
        )
    yield [last]


def ring_reduce(links, axis, count, me, own, sent, got, send_sem, recv_sem):
    last = count // 2
    for step in range(1, last + 1):
        yield step
        for h in range(2):
            for way, sign in enumerate((1, -1)):
                if step == 1 and h != way:
                    continue
                value = own(sign * (last + 1 - step), h)
                if step > 2 or (step == 2 and h == way):
                    links.arrived(
                        got.at[way, step - 1, h],
                        send_sem.at[way, step - 1, h],
                        recv_sem.at[way, step - 1, h],
                    )
                    value = value + got[way, step - 1, h].astype(F32)
                sent[way, step, h] = value.astype(BF16)
                links.send(
                    sent.at[way, step, h], got.at[way, step, h],
                    send_sem.at[way, step, h], recv_sem.at[way, step, h],
                    **{axis: wrap(me + sign, count)},
                )
    for h in range(2):
        for way in range(2):
            links.arrived(
                got.at[way, last, h], send_sem.at[way, last, h], recv_sem.at[way, last, h]
            )


def drain(steps):
    for _ in steps:
        pass


def routing_table(routes, gates):
    lane = lax.broadcasted_iota(jnp.int32, (8, 128), 1)
    gate = jnp.zeros((8, 128), F32)
    named = jnp.zeros((8, 128), F32)
    for k in range(TOP):
        expert = routes[:, k : k + 1]
        gate = gate + jnp.where(expert == lane, gates[:, k : k + 1], 0.0)
        named = named + jnp.where(expert == lane - 32, 1.0, 0.0)
    row = lax.broadcasted_iota(jnp.int32, (8, 8), 0)
    col = lax.broadcasted_iota(jnp.int32, (8, 8), 1)
    before = jnp.dot((col < row).astype(F32), named, preferred_element_type=F32)
    return jnp.where(lane < 32, gate, jnp.where(named > 0.5, before, UNNAMED))


def matches(table, z):
    lane = lax.broadcasted_iota(jnp.int32, (128, 128), 1)
    row = lax.broadcasted_iota(jnp.int32, (128, NX * HALF), 1)
    token = lax.broadcasted_iota(jnp.int32, (128, NX * HALF), 0)
    slot = jnp.zeros((128, NX * HALF), F32)
    gate = jnp.zeros((128, NX * HALF), F32)
    for k in range(NX):
        expert = z * NX + k
        gate_col = jnp.sum(jnp.where(lane == expert, table, 0.0), axis=1, keepdims=True)
        slot_col = jnp.sum(jnp.where(lane == expert + 32, table, 0.0), axis=1, keepdims=True)
        mine = jnp.logical_and(row >= k * HALF, row < (k + 1) * HALF)
        slot = jnp.where(mine, slot_col, slot)
        gate = jnp.where(mine, gate_col, gate)
    inner = lax.rem(row, HALF)
    hit = jnp.logical_and(
        lax.div(token, 8) == lax.div(inner, CAP), slot == lax.rem(inner, CAP).astype(F32)
    )
    return jnp.where(hit, 1.0, 0.0).astype(BF16), jnp.where(hit, gate, 0.0).astype(BF16)


def attend(g, s, anc, live, q, lat, vup, keys):
    width = (ANC + 1) * BLK
    col = lax.broadcasted_iota(jnp.int32, (2 * BLK, width), 1)
    row = lax.rem(lax.broadcasted_iota(jnp.int32, (2 * BLK, width), 0), BLK)
    for a in range(ANC):
        keys[a * BLK : (a + 1) * BLK, :] = lat[jnp.maximum(anc[g, a], 0)]
    keys[ANC * BLK :, :] = lat[s * 4 + g]
    query = q[:, g * BLK : (g + 1) * BLK, :].reshape(2 * BLK, LAT + ROPE)
    scores = lax.dot_general(
        query, keys[...], (((1,), (1,)), ((), ())), preferred_element_type=F32
    ) * ((HD + ROPE) ** (-0.5))
    mask = jnp.logical_and(row >= col - ANC * BLK, live[g : g + 1, :] > 0.5)
    highest = jnp.max(jnp.where(mask, scores, MASKED), axis=1, keepdims=True)
    weights = jnp.where(mask, jnp.exp(scores - highest), 0.0)
    total = jnp.sum(weights, axis=1, keepdims=True)
    summed = jnp.dot(weights.astype(BF16), keys[:, :LAT], preferred_element_type=F32)
    latent = (summed / total).astype(BF16)
    return jnp.concatenate(
        [
            jnp.dot(latent[h * BLK : (h + 1) * BLK], vup[h], preferred_element_type=F32)
            for h in range(2)
        ],
        axis=1,
    ).astype(BF16)


def layer_kernel(
    anc, anc_rows, q, vup, routes, gates, res, gain, lat_in, outp, wg, wu, wd,
    out,
    lat, keys, meta, meta_all, res32, res_y, op_all, ho_a, ho_b, partial, a_sent, a_got,
    att, xrecv, hidden, squares, tokens, choose, combine, disp, rows, w_in, w_out,
    gsend, g_sent, g_got, act, dout, back, comb, c_sent, c_got, fin, orecv,
    loc, lat_s, lat_r, fwd_s, fwd_r, op_s, op_r, me_s, me_r, mz_s, mz_r, re_s, re_r,
    a1_s, a1_r, b1_s, b1_r, a2_s, a2_r, b2_s, b2_r, za_s, za_r, xa_s, xa_r, sq_s, sq_r,
    tk_s, tk_r, dp_s, dp_r, w_s, w_r, f_s, f_r, gy_s, gy_r, ac_s, ac_r, bk_s, bk_r,
    zc_s, zc_r, fo_s, fo_r,
):
    y, c, z, x = place()
    s = y * 2 + c
    other = 1 - c
    links = Links(y, c, z, x)
    send, arrived = links.send, links.arrived

    def weight_source(k, to):
        at = pl.ds(pl.multiple_of(to * DY, 128), DY)
        return (wg.at[at, :], wu.at[at, :], wd.at[:, at])[k]

    def weight_place(k, src):
        if k == 2:
            return w_out.at[pl.ds(pl.multiple_of(src * 128, 128), 128), :]
        return w_in.at[:, pl.ds(pl.multiple_of(k * FF + src * 128, 128), 128)]

    def op_columns(to):
        start = pl.multiple_of(y * DY + jnp.minimum(to * CW, DY - CW), 128)
        return outp.at[:, pl.ds(start, CW)]

    own = [
        pltpu.make_async_copy(lat_in, lat.at[pl.ds(s * 4, 4)], loc.at[0]),
        pltpu.make_async_copy(op_columns(x), op_all.at[x], loc.at[1]),
    ] + [
        pltpu.make_async_copy(weight_source(k, y), weight_place(k, s), loc.at[2 + k])
        for k in range(3)
    ]
    for copy in own:
        copy.start()
    meta[...] = routing_table(routes[...], gates[...])
    meta_all[1, y] = meta[...]
    res32[...] = res[...].astype(F32)
    meet(
        [(wrap(y + d, NY), c, z, x) for d in range(1, NY)]
        + [(y, c, wrap(z + d, NZ), x) for d in range(1, NZ)]
        + [(y, c, z, wrap(x + d, NX)) for d in range(1, NX)]
        + [(y, other, z, x)]
    )

    own[0].wait()

    def lat_view(k, shift):
        return lat.at[pl.ds((wrap(y + k, NY) * 2 + c) * 4, 4)]

    lat_ring = ring_gather(
        links, "y", NY, y, lat_view, lambda ref, h: ref.at[pl.ds(h * 2, 2)], lat_s, lat_r
    )

    def forward(k):
        block = lat_view(k, 0)
        send(block, block, fwd_s.at[k % NY], fwd_r.at[k % NY], c=other)

    for d in range(1, NY):
        to = wrap(y + d, NY)
        send(meta, meta_all.at[1, y], me_s.at[d], me_r.at[d], y=to)
    first = next(lat_ring)
    forward(0)
    for k in first:
        forward(k)
    for d in range(1, NY):
        to = wrap(y + d, NY)
        part = res32.at[:, pl.ds(pl.multiple_of(to * DY, 128), DY)]
        send(part, res_y.at[y], re_s.at[d], re_r.at[d], y=to)
    for d in range(1, NX):
        to = wrap(x + d, NX)
        send(op_columns(to), op_all.at[x], op_s.at[d], op_r.at[d], x=to)
    for d in range(1, NY):
        arrived(meta_all.at[1, wrap(y - d, NY)], me_s.at[d], me_r.at[d])
    for d in range(1, NZ):
        send(meta_all.at[1], meta_all.at[(d + 1) % NZ], mz_s.at[d], mz_r.at[d], z=wrap(z + d, NZ))
    res_y[y] = res32[:, pl.ds(pl.multiple_of(y * DY, 128), DY)]
    area = lax.broadcasted_iota(jnp.int32, (ANC, (ANC + 1) * BLK), 1)
    slot_of = lax.broadcasted_iota(jnp.int32, (ANC, (ANC + 1) * BLK), 0)
    spread = (lax.div(area, BLK) == slot_of).astype(F32)
    live = jnp.dot((anc_rows[...] >= 0).astype(F32), spread, preferred_element_type=F32) + (
        lax.broadcasted_iota(jnp.int32, (4, (ANC + 1) * BLK), 1) >= ANC * BLK
    ).astype(F32)
    for new in lat_ring:
        for k in new:
            forward(k)
    for k in range(3):
        send(
            weight_source(k, y), weight_place(k, s), f_s.at[k, 0], f_r.at[k, 0], c=other
        )
    for d in (1, 3):
        to = wrap(y + d, NY)
        send(weight_source(2, to), weight_place(2, s), w_s.at[2, d], w_r.at[2, d], y=to)
    for k in range(NY):
        block = lat.at[pl.ds((wrap(y + k, NY) * 2 + other) * 4, 4)]
        arrived(block, fwd_s.at[k], fwd_r.at[k])

    for g in range(2):
        ho_a[y, x, g * BLK : (g + 1) * BLK, :] = attend(g, s, anc, live, q, lat, vup, keys)
    for d in range(1, NX):
        send(ho_a.at[y, x], ho_a.at[y, x], a1_s.at[d], a1_r.at[d], x=wrap(x + d, NX))
    for g in range(2):
        ho_b[x, y, g * BLK : (g + 1) * BLK, :] = attend(g + 2, s, anc, live, q, lat, vup, keys)
    for d in range(1, NY):
        send(ho_b.at[x, y], ho_b.at[x, y], b1_s.at[d], b1_r.at[d], y=wrap(y + d, NY))

    def pairs(ref, h):
        return ref.at[pl.ds(h * 2, 2)]

    a_ring = ring_gather(
        links, "y", NY, y, lambda k, shift: ho_a.at[wrap(y + k, NY)], pairs, a2_s, a2_r
    )
    b_ring = ring_gather(
        links, "x", NX, x, lambda k, shift: ho_b.at[wrap(x + k, NX)], pairs, b2_s, b2_r
    )
    for d in range(1, NX):
        arrived(ho_a.at[y, wrap(x - d, NX)], a1_s.at[d], a1_r.at[d])
    for d in range(1, NY):
        arrived(ho_b.at[x, wrap(y - d, NY)], b1_s.at[d], b1_r.at[d])
    next(a_ring)
    next(b_ring)
    for d in range(1, NZ):
        arrived(meta_all.at[(d + 1) % NZ], mz_s.at[d], mz_r.at[d])
    for h in range(2):
        pick, weigh = matches(meta_all[4 * h : 4 * h + 4].reshape(128, 128), z)
        choose[h] = pick
        combine[h] = weigh
    for d in range(1, NX):
        arrived(op_all.at[wrap(x - d, NX)], op_s.at[d], op_r.at[d])
    own[1].wait()
    drain(a_ring)
    drain(b_ring)
    for k in range(2):
        for d in (1, 3):
            to = wrap(y + d, NY)
            send(weight_source(k, to), weight_place(k, s), w_s.at[k, d], w_r.at[k, d], y=to)

    for n in range(NY):
        for low, block in ((0, lambda k: ho_a[n, k]), (4, lambda k: ho_b[k, n])):
            total = None
            for k in range(NX):
                part = jnp.dot(block(k), op_all[k], preferred_element_type=F32)
                total = part if total is None else total + part
            total = total.astype(BF16)
            for k in range(4):
                partial[low + k, n] = total[k * 32 : (k + 1) * 32]

    def attention_term(k, h):
        return partial[wrap(z + k, NZ), 2 * h : 2 * h + 2].astype(F32)

    drain(ring_reduce(links, "z", NZ, z, attention_term, a_sent, a_got, za_s, za_r))
    for h in range(2):
        total = (
            attention_term(0, h)
            + a_got[0, NZ // 2, h].astype(F32)
            + a_got[1, NZ // 2, h].astype(F32)
        )
        for k in range(NX):
            att[k, 2 * h : 2 * h + 2] = total[:, k * 8 : (k + 1) * 8]
    for d in range(1, NX):
        to = wrap(x + d, NX)
        send(att.at[to], xrecv.at[x], xa_s.at[d], xa_r.at[d], x=to)
    xrecv[x] = att[x]
    to = wrap(y + 2, NY)
    for k in range(3):
        send(weight_source(k, to), weight_place(k, s), w_s.at[k, 2], w_r.at[k, 2], y=to)
    for d in range(1, NY):
        arrived(res_y.at[wrap(y - d, NY)], re_s.at[d], re_r.at[d])
    for d in range(1, NX):
        arrived(xrecv.at[wrap(x - d, NX)], xa_s.at[d], xa_r.at[d])
    for k in range(NX):
        low = NX * CW - DY if k == NX - 1 else 0
        at, wide = k * CW, CW - low
        hidden[:, at : at + wide] = xrecv[k].reshape(NY * 8, CW)[:, low:] + res_y[
            :, :, at : at + wide
        ].reshape(NY * 8, wide)
    held = hidden[...]
    squares[y] = jnp.broadcast_to(jnp.sum(held * held, axis=1, keepdims=True), (NY * 8, 128))
    for d in range(1, NY):
        send(squares.at[y], squares.at[y], sq_s.at[d], sq_r.at[d], y=wrap(y + d, NY))
    for d in range(1, NY):
        arrived(squares.at[wrap(y - d, NY)], sq_s.at[d], sq_r.at[d])
    mean = (squares[0] + squares[1] + squares[2] + squares[3])[:, :1] * (1.0 / D)
    tokens[1] = (held * lax.rsqrt(mean + NORM_EPS) * gain[y]).astype(BF16)
    token_ring = ring_gather(
        links, "z", NZ, z,
        lambda k, shift: tokens.at[(1 - k + shift) % NZ],
        lambda ref, h: ref.at[pl.ds(h * 16, 16)],
        tk_s, tk_r,
    )

    def dispatch(h):
        table = tokens[4 * h : 4 * h + 4].reshape(128, DY)
        chosen = lax.dot_general(
            choose[h], table, (((0,), (0,)), ((), ())), preferred_element_type=F32
        ).astype(BF16)
        for k in range(NX):
            disp[h, k] = chosen[k * HALF : (k + 1) * HALF]
        for d in (2, 1, 3):
            to = wrap(x + d, NX)
            send(disp.at[h, to], rows.at[x, h], dp_s.at[h, d], dp_r.at[h, d], x=to)
        rows[x, h] = disp[h, x]

    def pass_on(k, d):
        block = weight_place(k, wrap(y - d, NY) * 2 + c)
        arrived(block, w_s.at[k, d], w_r.at[k, d])
        send(block, block, f_s.at[k, d], f_r.at[k, d], c=other)

    def from_other(k):
        own[2 + k].wait()
        for d in range(NY):
            block = weight_place(k, wrap(y - d, NY) * 2 + other)
            arrived(block, f_s.at[k, d], f_r.at[k, d])

    next(token_ring)
    next(token_ring)
    dispatch(0)
    next(token_ring)
    for k in (2, 0, 1):
        for d in (1, 3):
            pass_on(k, d)
    drain(token_ring)
    dispatch(1)
    for k in range(2):
        pass_on(k, 2)
    for k in range(2):
        from_other(k)

    for h in range(2):
        for d in range(1, NX):
            arrived(rows.at[wrap(x - d, NX), h], dp_s.at[h, d], dp_r.at[h, d])

        def inward(j, _):
            at = pl.ds(pl.multiple_of(j * 512, 512), 512)
            part = jnp.dot(
                rows[:, h].reshape(NX * HALF, DY), w_in[:, at], preferred_element_type=F32
            ).astype(BF16)
            for k in range(NX):
                gsend[k, h, :, at] = part[k * HALF : (k + 1) * HALF]
            return 0

        lax.fori_loop(0, 2 * FF // 512, inward, 0)

    def inward_term(k, h):
        return gsend[wrap(y + k, NY), h].astype(F32)

    drain(ring_reduce(links, "y", NY, y, inward_term, g_sent, g_got, gy_s, gy_r))
    for h in range(2):
        total = (
            inward_term(0, h)
            + g_got[0, NY // 2, h].astype(F32)
            + g_got[1, NY // 2, h].astype(F32)
        )
        gate = total[:, :FF]
        act[y, h] = (gate / (1.0 + jnp.exp(-gate)) * total[:, FF:]).astype(BF16)
    act_ring = ring_gather(
        links, "y", NY, y, lambda k, shift: act.at[wrap(y + k, NY)], lambda ref, h: ref.at[h],
        ac_s, ac_r,
    )
    next(act_ring)
    pass_on(2, 2)
    from_other(2)
    drain(act_ring)

    for h in (1, 0):
        def outward(j, _):
            at = pl.ds(pl.multiple_of(j * 256, 256), 256)
            part = jnp.dot(
                act[:, h].reshape(NX * HALF, FF), w_out[:, at], preferred_element_type=F32
            ).astype(BF16)
            for k in range(NX):
                dout[h, k, :, at] = part[k * HALF : (k + 1) * HALF]
            return 0

        lax.fori_loop(0, DY // 256, outward, 0)
        for d in (2, 1, 3):
            to = wrap(x + d, NX)
            send(dout.at[h, to], back.at[h, x], bk_s.at[h, d], bk_r.at[h, d], x=to)
        back[h, x] = dout[h, x]

    def weigh_rows(h):
        for d in range(1, NX):
            arrived(back.at[h, wrap(x - d, NX)], bk_s.at[h, d], bk_r.at[h, d])

        def gather(j, _):
            at = pl.ds(pl.multiple_of(j * 256, 256), 256)
            part = jnp.dot(
                combine[h], back[h, :, :, at].reshape(NX * HALF, 256), preferred_element_type=F32
            )
            for k in range(4):
                comb[4 * h + k, :, at] = part[k * 32 : (k + 1) * 32]
            return 0

        lax.fori_loop(0, DY // 256, gather, 0)

    def token_term(k, h):
        return comb[(1 - k) % NZ, h * 16 : (h + 1) * 16]

    weigh_rows(1)
    for step in ring_reduce(links, "z", NZ, z, token_term, c_sent, c_got, zc_s, zc_r):
        if step == 3:
            weigh_rows(0)
    for h in range(2):
        total = (
            hidden[h * 16 : (h + 1) * 16]
            + token_term(0, h)
            + c_got[0, NZ // 2, h].astype(F32)
            + c_got[1, NZ // 2, h].astype(F32)
        )
        fin[2 * h] = total[:8]
        fin[2 * h + 1] = total[8:]
    for d in (2, 1, 3):
        to = wrap(y + d, NY)
        send(fin.at[to], orecv.at[y], fo_s.at[d], fo_r.at[d], y=to)
    orecv[y] = fin[y]
    for d in range(1, NY):
        arrived(orecv.at[wrap(y - d, NY)], fo_s.at[d], fo_r.at[d])
    for k in range(NY):
        out[:, k * DY : (k + 1) * DY] = orecv[k]
    links.finish()


def layer(*operands):
    def two(*shape):
        return [DMA(shape), DMA(shape)]

    return pl.pallas_call(
        layer_kernel,
        out_shape=jax.ShapeDtypeStruct((8, D), F32),
        in_specs=[SMEM] + [VMEM] * 7 + [ANY] * 5,
        out_specs=VMEM,
        scratch_shapes=[
            pltpu.VMEM((32, BLK, LAT + ROPE), BF16),
            pltpu.VMEM(((ANC + 1) * BLK, LAT + ROPE), BF16),
            pltpu.VMEM((8, 128), F32),
            pltpu.VMEM((NZ, NY, 8, 128), F32),
            pltpu.VMEM((8, D), F32),
            pltpu.VMEM((NY, 8, DY), F32),
            pltpu.VMEM((NX, 256, CW), BF16),
            pltpu.VMEM((NY, NX, 128, 256), BF16),
            pltpu.VMEM((NX, NY, 128, 256), BF16),
            pltpu.VMEM((NZ, NY, 32, CW), BF16),
            pltpu.VMEM((2, NZ // 2 + 1, 2, 2, 32, CW), BF16),
            pltpu.VMEM((2, NZ // 2 + 1, 2, 2, 32, CW), BF16),
            pltpu.VMEM((NX, NY, 8, CW), F32),
            pltpu.VMEM((NX, NY, 8, CW), F32),
            pltpu.VMEM((NY * 8, DY), F32),
            pltpu.VMEM((NY, NY * 8, 128), F32),
            pltpu.VMEM((NZ, NY * 8, DY), BF16),
            pltpu.VMEM((2, 128, NX * HALF), BF16),
            pltpu.VMEM((2, 128, NX * HALF), BF16),
            pltpu.VMEM((2, NX, HALF, DY), BF16),
            pltpu.VMEM((NX, 2, HALF, DY), BF16),
            pltpu.VMEM((DY, 2 * FF), BF16),
            pltpu.VMEM((FF, DY), BF16),
            pltpu.VMEM((NY, 2, HALF, 2 * FF), BF16),
            pltpu.VMEM((2, NY // 2 + 1, 2, HALF, 2 * FF), BF16),
            pltpu.VMEM((2, NY // 2 + 1, 2, HALF, 2 * FF), BF16),
            pltpu.VMEM((NY, 2, HALF, FF), BF16),
            pltpu.VMEM((2, NX, HALF, DY), BF16),
            pltpu.VMEM((2, NX, HALF, DY), BF16),
            pltpu.VMEM((NZ, NY * 8, DY), F32),
            pltpu.VMEM((2, NZ // 2 + 1, 2, 16, DY), BF16),
            pltpu.VMEM((2, NZ // 2 + 1, 2, 16, DY), BF16),
            pltpu.VMEM((NY, 8, DY), F32),
            pltpu.VMEM((NY, 8, DY), F32),
            DMA((5,)),
            *two(2, NY // 2 + 1),
            *two(NY),
            *two(NX),
            *two(NY),
            *two(NZ),
            *two(NY),
            *two(NX),
            *two(NY),
            *two(2, NY // 2 + 1),
            *two(2, NX // 2 + 1),
            *two(2, NZ // 2 + 1, 2),
            *two(NX),
            *two(NY),
            *two(2, NZ // 2 + 1),
            *two(2, NX),
            *two(3, NY),
            *two(3, NY),
            *two(2, NY // 2 + 1, 2),
            *two(2, NY // 2 + 1),
            *two(2, NX),
            *two(2, NZ // 2 + 1, 2),
            *two(NY),
        ],
        compiler_params=pltpu.CompilerParams(
            collective_id=0, has_side_effects=True, vmem_limit_bytes=52 << 20
        ),
        name="layer",
    )(*operands)


def on_device(
    queries,
    latent_cache,
    ancestors,
    value_up,
    out_proj,
    residual,
    norm_gain,
    routes,
    gates,
    w_gate,
    w_up,
    w_down,
):
    final = layer(
        ancestors,
        ancestors,
        queries.transpose(1, 0, 2),
        value_up,
        routes,
        gates,
        residual,
        norm_gain.astype(F32).reshape(NY, 1, DY),
        latent_cache,
        out_proj,
        w_gate[0],
        w_up[0],
        w_down[0],
    )
    return final.astype(BF16)


def solution(mesh):
    placed = (
        P("seq", "exp", None),
        P("seq", None, None),
        P("seq", None),
        P("exp", None, None),
        P("exp", None),
        P(("seq", "exp"), None),
        P(),
        P(("seq", "exp"), None),
        P(("seq", "exp"), None),
        P("exp", None, "seq"),
        P("exp", None, "seq"),
        P("exp", "seq", None),
    )
    return jax.shard_map(
        on_device, mesh=mesh, in_specs=placed, out_specs=P(("seq", "exp"), None), check_vma=False
    )
```

```python
import jax
import jax.numpy as jnp
from jax import lax
from jax.experimental import pallas as pl
from jax.experimental.pallas import tpu as pltpu
from jax.sharding import PartitionSpec as P

D = 7168
LAT = 512
ROPE = 64
HD = 128
BLK = 64
ANC = 8
TOP = 8
CAP = 3
NY, NZ, NX = 4, 8, 4
DY = D // NY
CW = 512
FF = 1024
HALF = 48
UNNAMED = 99.0
NORM_EPS = 1e-6
MASKED = -1e30
F32 = jnp.float32
BF16 = jnp.bfloat16
ANY = pl.BlockSpec(memory_space=pl.ANY)
VMEM = pl.BlockSpec(memory_space=pltpu.VMEM)
SMEM = pl.BlockSpec(memory_space=pltpu.SMEM)
DMA = pltpu.SemaphoreType.DMA


def place():
    s = lax.axis_index("seq")
    e = lax.axis_index("exp")
    return lax.div(s, 2), lax.rem(s, 2), lax.div(e, NX), lax.rem(e, NX)


def wrap(value, count):
    return lax.rem(value + count, count)


def meet(peers):
    barrier = pltpu.get_barrier_semaphore()
    for y, c, z, x in peers:
        pl.semaphore_signal(
            barrier,
            inc=1,
            device_id=(y * 2 + c, z * NX + x),
            device_id_type=pl.DeviceIdType.MESH,
        )
    pl.semaphore_wait(barrier, len(peers))


class Links:
    def __init__(self, y, c, z, x):
        self.at = (y, c, z, x)
        self.started = []

    def copy(self, src, dst, send_sem, recv_sem, y=None, c=None, z=None, x=None):
        here = self.at
        y, c, z, x = (own if new is None else new for new, own in zip((y, c, z, x), here))
        return pltpu.make_async_remote_copy(
            src_ref=src,
            dst_ref=dst,
            send_sem=send_sem,
            recv_sem=recv_sem,
            device_id=(y * 2 + c, z * NX + x),
            device_id_type=pl.DeviceIdType.MESH,
        )

    def send(self, src, dst, send_sem, recv_sem, **to):
        copy = self.copy(src, dst, send_sem, recv_sem, **to)
        copy.start()
        self.started.append(copy)

    def arrived(self, dst, send_sem, recv_sem):
        self.copy(dst, dst, send_sem, recv_sem).wait_recv()

    def finish(self):
        for copy in self.started:
            copy.wait_send()


def ring_gather(links, axis, count, me, view, half, send_sem, recv_sem):
    last = count // 2

    def got(way, step, part):
        links.arrived(
            half(view(-(1, -1)[way] * step, 0), part),
            send_sem.at[way, step, part],
            recv_sem.at[way, step, part],
        )

    for step in range(1, last + 1):
        new = []
        for part_at in range(2):
            for way, sign in enumerate((1, -1)):
                part = way if part_at == 0 else 1 - way
                k = -sign * (step - 1)
                if step > 1:
                    got(way, step - 1, part)
                    if part_at:
                        new.append(k)
                if step < last or part == way:
                    links.send(
                        half(view(k, 0), part), half(view(k, sign), part),
                        send_sem.at[way, step, part], recv_sem.at[way, step, part],
                        **{axis: wrap(me + sign, count)},
                    )
        if new:
            yield new
    for way in range(2):
        got(way, last, way)
    yield [last]


def ring_reduce(links, axis, count, me, own, sent, got, send_sem, recv_sem):
    last = count // 2
    for step in range(1, last + 1):
        yield step
        for part_at in range(2):
            for way, sign in enumerate((1, -1)):
                h = 1 - way if part_at == 0 else way
                if step == 1 and h != way:
                    continue
                value = own(sign * (last + 1 - step), h)
                if step > 2 or (step == 2 and h == way):
                    links.arrived(
                        got.at[way, step - 1, h],
                        send_sem.at[way, step - 1, h],
                        recv_sem.at[way, step - 1, h],
                    )
                    value = value + got[way, step - 1, h].astype(F32)
                sent[way, step, h] = value.astype(BF16)
                links.send(
                    sent.at[way, step, h], got.at[way, step, h],
                    send_sem.at[way, step, h], recv_sem.at[way, step, h],
                    **{axis: wrap(me + sign, count)},
                )
    for h in range(2):
        for way in range(2):
            links.arrived(
                got.at[way, last, h], send_sem.at[way, last, h], recv_sem.at[way, last, h]
            )


def drain(steps):
    for _ in steps:
        pass


def routing_table(routes, gates):
    lane = lax.broadcasted_iota(jnp.int32, (8, 128), 1)
    gate = jnp.zeros((8, 128), F32)
    named = jnp.zeros((8, 128), F32)
    for k in range(TOP):
        expert = routes[:, k : k + 1]
        gate = gate + jnp.where(expert == lane, gates[:, k : k + 1], 0.0)
        named = named + jnp.where(expert == lane - 32, 1.0, 0.0)
    row = lax.broadcasted_iota(jnp.int32, (8, 8), 0)
    col = lax.broadcasted_iota(jnp.int32, (8, 8), 1)
    before = jnp.dot((col < row).astype(F32), named, preferred_element_type=F32)
    return jnp.where(lane < 32, gate, jnp.where(named > 0.5, before, UNNAMED))


def matches(table, z):
    lane = lax.broadcasted_iota(jnp.int32, (128, 128), 1)
    row = lax.broadcasted_iota(jnp.int32, (128, NX * HALF), 1)
    token = lax.broadcasted_iota(jnp.int32, (128, NX * HALF), 0)
    slot = jnp.zeros((128, NX * HALF), F32)
    gate = jnp.zeros((128, NX * HALF), F32)
    for k in range(NX):
        expert = z * NX + k
        gate_col = jnp.sum(jnp.where(lane == expert, table, 0.0), axis=1, keepdims=True)
        slot_col = jnp.sum(jnp.where(lane == expert + 32, table, 0.0), axis=1, keepdims=True)
        mine = jnp.logical_and(row >= k * HALF, row < (k + 1) * HALF)
        slot = jnp.where(mine, slot_col, slot)
        gate = jnp.where(mine, gate_col, gate)
    inner = lax.rem(row, HALF)
    hit = jnp.logical_and(
        lax.div(token, 8) == lax.div(inner, CAP), slot == lax.rem(inner, CAP).astype(F32)
    )
    return jnp.where(hit, 1.0, 0.0).astype(BF16), jnp.where(hit, gate, 0.0).astype(BF16)


def attend(g, s, anc, live, q, lat, vup, keys):
    width = (ANC + 1) * BLK
    col = lax.broadcasted_iota(jnp.int32, (2 * BLK, width), 1)
    row = lax.rem(lax.broadcasted_iota(jnp.int32, (2 * BLK, width), 0), BLK)
    for a in range(ANC):
        keys[a * BLK : (a + 1) * BLK, :] = lat[jnp.maximum(anc[g, a], 0)]
    keys[ANC * BLK :, :] = lat[s * 4 + g]
    query = q[:, g * BLK : (g + 1) * BLK, :].reshape(2 * BLK, LAT + ROPE)
    scores = lax.dot_general(
        query, keys[...], (((1,), (1,)), ((), ())), preferred_element_type=F32
    ) * ((HD + ROPE) ** (-0.5))
    mask = jnp.logical_and(row >= col - ANC * BLK, live[g : g + 1, :] > 0.5)
    highest = jnp.max(jnp.where(mask, scores, MASKED), axis=1, keepdims=True)
    weights = jnp.where(mask, jnp.exp(scores - highest), 0.0)
    total = jnp.sum(weights, axis=1, keepdims=True)
    summed = jnp.dot(weights.astype(BF16), keys[:, :LAT], preferred_element_type=F32)
    latent = (summed / total).astype(BF16)
    return jnp.concatenate(
        [
            jnp.dot(latent[h * BLK : (h + 1) * BLK], vup[h], preferred_element_type=F32)
            for h in range(2)
        ],
        axis=1,
    ).astype(BF16)


def layer_kernel(
    anc, q_in, vup_in, gates_in, res_in, routes_in, anc_in, gain_in, lat_in, outp, wg, wu, wd,
    out,
    q, vup, gates, res, routes, anc_rows, gain,
    lat, keys, meta, meta_all, res32, res_y, op_all, ho_a, ho_b, partial, a_sent, a_got,
    att, xrecv, hidden, squares, tokens, choose, combine, disp, rows, w_in, w_out,
    gsend, g_sent, g_got, act, dout, back, comb, c_sent, c_got, fin, orecv,
    loc, lat_s, lat_r, fwd_s, fwd_r, op_s, op_r, me_s, me_r, mz_s, mz_r, re_s, re_r,
    a1_s, a1_r, b1_s, b1_r, a2_s, a2_r, b2_s, b2_r, za_s, za_r, xa_s, xa_r, sq_s, sq_r,
    tk_s, tk_r, dp_s, dp_r, w_s, w_r, f_s, f_r, gy_s, gy_r, ac_s, ac_r, bk_s, bk_r,
    zc_s, zc_r, fo_s, fo_r,
):
    y, c, z, x = place()
    s = y * 2 + c
    other = 1 - c
    links = Links(y, c, z, x)
    send, arrived = links.send, links.arrived

    def weight_source(k, to):
        at = pl.ds(pl.multiple_of(to * DY, 128), DY)
        return (wg.at[at, :], wu.at[at, :], wd.at[:, at])[k]

    def weight_place(k, src):
        if k == 2:
            return w_out.at[pl.ds(pl.multiple_of(src * 128, 128), 128), :]
        return w_in.at[:, pl.ds(pl.multiple_of(k * FF + src * 128, 128), 128)]

    def send_weights(k, d):
        to = wrap(y + d, NY)
        send(weight_source(k, to), weight_place(k, s), w_s.at[k, d], w_r.at[k, d], y=to)

    def pass_on(k, d):
        block = weight_place(k, wrap(y - d, NY) * 2 + c)
        arrived(block, w_s.at[k, d], w_r.at[k, d])
        send(block, block, f_s.at[k, d], f_r.at[k, d], c=other)

    def from_other(k):
        own[2 + k].wait()
        for d in range(NY):
            block = weight_place(k, wrap(y - d, NY) * 2 + other)
            arrived(block, f_s.at[k, d], f_r.at[k, d])

    def op_columns(to):
        start = pl.multiple_of(y * DY + jnp.minimum(to * CW, DY - CW), 128)
        return outp.at[:, pl.ds(start, CW)]

    own = [
        pltpu.make_async_copy(lat_in, lat.at[pl.ds(s * 4, 4)], loc.at[0]),
        pltpu.make_async_copy(op_columns(x), op_all.at[x], loc.at[1]),
    ] + [
        pltpu.make_async_copy(weight_source(k, y), weight_place(k, s), loc.at[2 + k])
        for k in range(3)
    ]
    small = [
        pltpu.make_async_copy(src, dst, loc.at[5 + k])
        for k, (src, dst) in enumerate(
            (
                (routes_in, routes),
                (gates_in, gates),
                (res_in, res),
                (anc_in, anc_rows),
                (gain_in, gain),
                (q_in, q),
                (vup_in, vup),
            )
        )
    ]
    for copy in own[:1] + small + own[1:]:
        copy.start()
    for copy in small[:3]:
        copy.wait()
    meta[...] = routing_table(routes[...], gates[...])
    meta_all[1, y] = meta[...]
    res32[...] = res[...].astype(F32)
    meet(
        [(wrap(y + d, NY), c, z, x) for d in range(1, NY)]
        + [(y, c, wrap(z + d, NZ), x) for d in range(1, NZ)]
        + [(y, c, z, wrap(x + d, NX)) for d in range(1, NX)]
        + [(y, other, z, x)]
    )

    own[0].wait()

    def lat_view(k, shift):
        return lat.at[pl.ds((wrap(y + k, NY) * 2 + c) * 4, 4)]

    lat_ring = ring_gather(
        links, "y", NY, y, lat_view, lambda ref, h: ref.at[pl.ds(h * 2, 2)], lat_s, lat_r
    )

    def forward(k):
        block = lat_view(k, 0)
        send(block, block, fwd_s.at[k % NY], fwd_r.at[k % NY], c=other)

    for d in range(1, NY):
        to = wrap(y + d, NY)
        send(meta, meta_all.at[1, y], me_s.at[d], me_r.at[d], y=to)
    first = next(lat_ring)
    forward(0)
    for k in first:
        forward(k)
    for k in range(2):
        for d in (1, 3):
            send_weights(k, d)
    for d in range(1, NX):
        to = wrap(x + d, NX)
        send(op_columns(to), op_all.at[x], op_s.at[d], op_r.at[d], x=to)
    for d in range(1, NY):
        arrived(meta_all.at[1, wrap(y - d, NY)], me_s.at[d], me_r.at[d])
    for d in range(1, NZ):
        send(meta_all.at[1], meta_all.at[(d + 1) % NZ], mz_s.at[d], mz_r.at[d], z=wrap(z + d, NZ))
    res_y[y] = res32[:, pl.ds(pl.multiple_of(y * DY, 128), DY)]
    for copy in small[3:]:
        copy.wait()
    area = lax.broadcasted_iota(jnp.int32, (ANC, (ANC + 1) * BLK), 1)
    slot_of = lax.broadcasted_iota(jnp.int32, (ANC, (ANC + 1) * BLK), 0)
    spread = (lax.div(area, BLK) == slot_of).astype(F32)
    live = jnp.dot((anc_rows[...] >= 0).astype(F32), spread, preferred_element_type=F32) + (
        lax.broadcasted_iota(jnp.int32, (4, (ANC + 1) * BLK), 1) >= ANC * BLK
    ).astype(F32)
    for new in lat_ring:
        for k in new:
            forward(k)
    for k in range(3):
        send(
            weight_source(k, y), weight_place(k, s), f_s.at[k, 0], f_r.at[k, 0], c=other
        )
    for k in range(NY):
        block = lat.at[pl.ds((wrap(y + k, NY) * 2 + other) * 4, 4)]
        arrived(block, fwd_s.at[k], fwd_r.at[k])

    for g in range(2):
        ho_a[y, x, g * BLK : (g + 1) * BLK, :] = attend(g, s, anc, live, q, lat, vup, keys)
    for d in range(1, NX):
        send(ho_a.at[y, x], ho_a.at[y, x], a1_s.at[d], a1_r.at[d], x=wrap(x + d, NX))
    for g in range(2):
        ho_b[x, y, g * BLK : (g + 1) * BLK, :] = attend(g + 2, s, anc, live, q, lat, vup, keys)
    for d in range(1, NY):
        send(ho_b.at[x, y], ho_b.at[x, y], b1_s.at[d], b1_r.at[d], y=wrap(y + d, NY))

    def pairs(ref, h):
        return ref.at[pl.ds(h * 2, 2)]

    a_ring = ring_gather(
        links, "y", NY, y, lambda k, shift: ho_a.at[wrap(y + k, NY)], pairs, a2_s, a2_r
    )
    b_ring = ring_gather(
        links, "x", NX, x, lambda k, shift: ho_b.at[wrap(x + k, NX)], pairs, b2_s, b2_r
    )
    for d in range(1, NX):
        arrived(ho_a.at[y, wrap(x - d, NX)], a1_s.at[d], a1_r.at[d])
    for d in range(1, NY):
        arrived(ho_b.at[x, wrap(y - d, NY)], b1_s.at[d], b1_r.at[d])
    next(a_ring)
    next(b_ring)
    for d in range(1, NZ):
        arrived(meta_all.at[(d + 1) % NZ], mz_s.at[d], mz_r.at[d])
    for h in range(2):
        pick, weigh = matches(meta_all[4 * h : 4 * h + 4].reshape(128, 128), z)
        choose[h] = pick
        combine[h] = weigh
    for d in range(1, NX):
        arrived(op_all.at[wrap(x - d, NX)], op_s.at[d], op_r.at[d])
    own[1].wait()
    drain(a_ring)
    drain(b_ring)
    for d in range(1, NY):
        to = wrap(y + d, NY)
        part = res32.at[:, pl.ds(pl.multiple_of(to * DY, 128), DY)]
        send(part, res_y.at[y], re_s.at[d], re_r.at[d], y=to)
    send_weights(0, 2)
    send_weights(1, 2)
    for k in range(2):
        for d in (1, 3):
            pass_on(k, d)

    for n in range(NY):
        for low, block in ((0, lambda k: ho_a[n, k]), (4, lambda k: ho_b[k, n])):
            total = None
            for k in range(NX):
                part = jnp.dot(block(k), op_all[k], preferred_element_type=F32)
                total = part if total is None else total + part
            total = total.astype(BF16)
            for k in range(4):
                partial[low + k, n] = total[k * 32 : (k + 1) * 32]

    def attention_term(k, h):
        return partial[wrap(z + k, NZ), 2 * h : 2 * h + 2].astype(F32)

    drain(ring_reduce(links, "z", NZ, z, attention_term, a_sent, a_got, za_s, za_r))
    for h in range(2):
        total = (
            attention_term(0, h)
            + a_got[0, NZ // 2, h].astype(F32)
            + a_got[1, NZ // 2, h].astype(F32)
        )
        for k in range(NX):
            att[k, 2 * h : 2 * h + 2] = total[:, k * 8 : (k + 1) * 8]
    for d in range(1, NX):
        to = wrap(x + d, NX)
        send(att.at[to], xrecv.at[x], xa_s.at[d], xa_r.at[d], x=to)
    xrecv[x] = att[x]
    for d in range(1, NY):
        arrived(res_y.at[wrap(y - d, NY)], re_s.at[d], re_r.at[d])
    for d in range(1, NX):
        arrived(xrecv.at[wrap(x - d, NX)], xa_s.at[d], xa_r.at[d])
    for k in range(NX):
        low = NX * CW - DY if k == NX - 1 else 0
        at, wide = k * CW, CW - low
        hidden[:, at : at + wide] = xrecv[k].reshape(NY * 8, CW)[:, low:] + res_y[
            :, :, at : at + wide
        ].reshape(NY * 8, wide)
    held = hidden[...]
    squares[y] = jnp.broadcast_to(jnp.sum(held * held, axis=1, keepdims=True), (NY * 8, 128))
    for d in range(1, NY):
        send(squares.at[y], squares.at[y], sq_s.at[d], sq_r.at[d], y=wrap(y + d, NY))
    for d in range(1, NY):
        arrived(squares.at[wrap(y - d, NY)], sq_s.at[d], sq_r.at[d])
    for d in (1, 3, 2):
        send_weights(2, d)
    mean = (squares[0] + squares[1] + squares[2] + squares[3])[:, :1] * (1.0 / D)
    tokens[1] = (held * lax.rsqrt(mean + NORM_EPS) * gain[y]).astype(BF16)
    token_ring = ring_gather(
        links, "z", NZ, z,
        lambda k, shift: tokens.at[(1 - k + shift) % NZ],
        lambda ref, h: ref.at[pl.ds(h * 16, 16)],
        tk_s, tk_r,
    )

    def dispatch(h):
        table = tokens[4 * h : 4 * h + 4].reshape(128, DY)
        chosen = lax.dot_general(
            choose[h], table, (((0,), (0,)), ((), ())), preferred_element_type=F32
        ).astype(BF16)
        for k in range(NX):
            disp[h, k] = chosen[k * HALF : (k + 1) * HALF]
        for d in (2, 1, 3):
            to = wrap(x + d, NX)
            send(disp.at[h, to], rows.at[x, h], dp_s.at[h, d], dp_r.at[h, d], x=to)
        rows[x, h] = disp[h, x]

    next(token_ring)
    next(token_ring)
    dispatch(0)
    next(token_ring)
    for k in range(2):
        pass_on(k, 2)
    drain(token_ring)
    dispatch(1)
    for k in range(2):
        from_other(k)

    for h in range(2):
        for d in range(1, NX):
            arrived(rows.at[wrap(x - d, NX), h], dp_s.at[h, d], dp_r.at[h, d])

        def inward(j, _):
            at = pl.ds(pl.multiple_of(j * 512, 512), 512)
            part = jnp.dot(
                rows[:, h].reshape(NX * HALF, DY), w_in[:, at], preferred_element_type=F32
            ).astype(BF16)
            for k in range(NX):
                gsend[k, h, :, at] = part[k * HALF : (k + 1) * HALF]
            return 0

        lax.fori_loop(0, 2 * FF // 512, inward, 0)

    def inward_term(k, h):
        return gsend[wrap(y + k, NY), h].astype(F32)

    drain(ring_reduce(links, "y", NY, y, inward_term, g_sent, g_got, gy_s, gy_r))
    for h in range(2):
        total = (
            inward_term(0, h)
            + g_got[0, NY // 2, h].astype(F32)
            + g_got[1, NY // 2, h].astype(F32)
        )
        gate = total[:, :FF]
        act[y, h] = (gate / (1.0 + jnp.exp(-gate)) * total[:, FF:]).astype(BF16)
    act_ring = ring_gather(
        links, "y", NY, y, lambda k, shift: act.at[wrap(y + k, NY)], lambda ref, h: ref.at[h],
        ac_s, ac_r,
    )
    next(act_ring)
    for d in (1, 3, 2):
        pass_on(2, d)
    from_other(2)
    drain(act_ring)

    for h in (1, 0):
        def outward(j, _):
            at = pl.ds(pl.multiple_of(j * 256, 256), 256)
            part = jnp.dot(
                act[:, h].reshape(NX * HALF, FF), w_out[:, at], preferred_element_type=F32
            ).astype(BF16)
            for k in range(NX):
                dout[h, k, :, at] = part[k * HALF : (k + 1) * HALF]
            return 0

        lax.fori_loop(0, DY // 256, outward, 0)
        for d in (2, 1, 3):
            to = wrap(x + d, NX)
            send(dout.at[h, to], back.at[h, x], bk_s.at[h, d], bk_r.at[h, d], x=to)
        back[h, x] = dout[h, x]

    def weigh_rows(h):
        for d in range(1, NX):
            arrived(back.at[h, wrap(x - d, NX)], bk_s.at[h, d], bk_r.at[h, d])

        def gather(j, _):
            at = pl.ds(pl.multiple_of(j * 256, 256), 256)
            part = jnp.dot(
                combine[h], back[h, :, :, at].reshape(NX * HALF, 256), preferred_element_type=F32
            )
            for k in range(4):
                comb[4 * h + k, :, at] = part[k * 32 : (k + 1) * 32]
            return 0

        lax.fori_loop(0, DY // 256, gather, 0)

    def token_term(k, h):
        return comb[(1 - k) % NZ, h * 16 : (h + 1) * 16]

    weigh_rows(1)
    for step in ring_reduce(links, "z", NZ, z, token_term, c_sent, c_got, zc_s, zc_r):
        if step == 3:
            weigh_rows(0)
    for h in range(2):
        total = (
            hidden[h * 16 : (h + 1) * 16]
            + token_term(0, h)
            + c_got[0, NZ // 2, h].astype(F32)
            + c_got[1, NZ // 2, h].astype(F32)
        )
        fin[2 * h] = total[:8]
        fin[2 * h + 1] = total[8:]
    for d in (2, 1, 3):
        to = wrap(y + d, NY)
        send(fin.at[to], orecv.at[y], fo_s.at[d], fo_r.at[d], y=to)
    orecv[y] = fin[y]
    for d in range(1, NY):
        arrived(orecv.at[wrap(y - d, NY)], fo_s.at[d], fo_r.at[d])
    for k in range(NY):
        out[:, k * DY : (k + 1) * DY] = orecv[k]
    links.finish()


def layer(*operands):
    def two(*shape):
        return [DMA(shape), DMA(shape)]

    return pl.pallas_call(
        layer_kernel,
        out_shape=jax.ShapeDtypeStruct((8, D), F32),
        in_specs=[SMEM] + [ANY] * 12,
        out_specs=VMEM,
        scratch_shapes=[
            pltpu.VMEM((2, 256, LAT + ROPE), BF16),
            pltpu.VMEM((2, LAT, HD), BF16),
            pltpu.VMEM((8, TOP), F32),
            pltpu.VMEM((8, D), BF16),
            pltpu.VMEM((8, TOP), jnp.int32),
            pltpu.VMEM((4, ANC), jnp.int32),
            pltpu.VMEM((NY, 1, DY), F32),
            pltpu.VMEM((32, BLK, LAT + ROPE), BF16),
            pltpu.VMEM(((ANC + 1) * BLK, LAT + ROPE), BF16),
            pltpu.VMEM((8, 128), F32),
            pltpu.VMEM((NZ, NY, 8, 128), F32),
            pltpu.VMEM((8, D), F32),
            pltpu.VMEM((NY, 8, DY), F32),
            pltpu.VMEM((NX, 256, CW), BF16),
            pltpu.VMEM((NY, NX, 128, 256), BF16),
            pltpu.VMEM((NX, NY, 128, 256), BF16),
            pltpu.VMEM((NZ, NY, 32, CW), BF16),
            pltpu.VMEM((2, NZ // 2 + 1, 2, 2, 32, CW), BF16),
            pltpu.VMEM((2, NZ // 2 + 1, 2, 2, 32, CW), BF16),
            pltpu.VMEM((NX, NY, 8, CW), F32),
            pltpu.VMEM((NX, NY, 8, CW), F32),
            pltpu.VMEM((NY * 8, DY), F32),
            pltpu.VMEM((NY, NY * 8, 128), F32),
            pltpu.VMEM((NZ, NY * 8, DY), BF16),
            pltpu.VMEM((2, 128, NX * HALF), BF16),
            pltpu.VMEM((2, 128, NX * HALF), BF16),
            pltpu.VMEM((2, NX, HALF, DY), BF16),
            pltpu.VMEM((NX, 2, HALF, DY), BF16),
            pltpu.VMEM((DY, 2 * FF), BF16),
            pltpu.VMEM((FF, DY), BF16),
            pltpu.VMEM((NY, 2, HALF, 2 * FF), BF16),
            pltpu.VMEM((2, NY // 2 + 1, 2, HALF, 2 * FF), BF16),
            pltpu.VMEM((2, NY // 2 + 1, 2, HALF, 2 * FF), BF16),
            pltpu.VMEM((NY, 2, HALF, FF), BF16),
            pltpu.VMEM((2, NX, HALF, DY), BF16),
            pltpu.VMEM((2, NX, HALF, DY), BF16),
            pltpu.VMEM((NZ, NY * 8, DY), F32),
            pltpu.VMEM((2, NZ // 2 + 1, 2, 16, DY), BF16),
            pltpu.VMEM((2, NZ // 2 + 1, 2, 16, DY), BF16),
            pltpu.VMEM((NY, 8, DY), F32),
            pltpu.VMEM((NY, 8, DY), F32),
            DMA((12,)),
            *two(2, NY // 2 + 1, 2),
            *two(NY),
            *two(NX),
            *two(NY),
            *two(NZ),
            *two(NY),
            *two(NX),
            *two(NY),
            *two(2, NY // 2 + 1, 2),
            *two(2, NX // 2 + 1, 2),
            *two(2, NZ // 2 + 1, 2),
            *two(NX),
            *two(NY),
            *two(2, NZ // 2 + 1, 2),
            *two(2, NX),
            *two(3, NY),
            *two(3, NY),
            *two(2, NY // 2 + 1, 2),
            *two(2, NY // 2 + 1, 2),
            *two(2, NX),
            *two(2, NZ // 2 + 1, 2),
            *two(NY),
        ],
        compiler_params=pltpu.CompilerParams(
            collective_id=0, has_side_effects=True, vmem_limit_bytes=63 << 20
        ),
        name="layer",
    )(*operands)


def on_device(
    queries,
    latent_cache,
    ancestors,
    value_up,
    out_proj,
    residual,
    norm_gain,
    routes,
    gates,
    w_gate,
    w_up,
    w_down,
):
    final = layer(
        ancestors,
        queries.transpose(1, 0, 2),
        value_up,
        gates,
        residual,
        routes,
        ancestors,
        norm_gain.astype(F32).reshape(NY, 1, DY),
        latent_cache,
        out_proj,
        w_gate[0],
        w_up[0],
        w_down[0],
    )
    return final.astype(BF16)


def solution(mesh):
    placed = (
        P("seq", "exp", None),
        P("seq", None, None),
        P("seq", None),
        P("exp", None, None),
        P("exp", None),
        P(("seq", "exp"), None),
        P(),
        P(("seq", "exp"), None),
        P(("seq", "exp"), None),
        P("exp", None, "seq"),
        P("exp", None, "seq"),
        P("exp", "seq", None),
    )
    return jax.shard_map(
        on_device, mesh=mesh, in_specs=placed, out_specs=P(("seq", "exp"), None), check_vma=False
    )
```

```python
import jax
import jax.numpy as jnp
from jax import lax
from jax.experimental import pallas as pl
from jax.experimental.pallas import tpu as pltpu
from jax.sharding import PartitionSpec as P

D = 7168
LAT = 512
ROPE = 64
HD = 128
BLK = 64
ANC = 8
TOP = 8
CAP = 3
NY, NZ, NX = 4, 8, 4
DY = D // NY
CW = 512
FF = 1024
HALF = 48
UNNAMED = 99.0
NORM_EPS = 1e-6
MASKED = -1e30
F32 = jnp.float32
BF16 = jnp.bfloat16
ANY = pl.BlockSpec(memory_space=pl.ANY)
VMEM = pl.BlockSpec(memory_space=pltpu.VMEM)
SMEM = pl.BlockSpec(memory_space=pltpu.SMEM)
DMA = pltpu.SemaphoreType.DMA


def place():
    s = lax.axis_index("seq")
    e = lax.axis_index("exp")
    return lax.div(s, 2), lax.rem(s, 2), lax.div(e, NX), lax.rem(e, NX)


def wrap(value, count):
    return lax.rem(value + count, count)


def meet(peers):
    barrier = pltpu.get_barrier_semaphore()
    for y, c, z, x in peers:
        pl.semaphore_signal(
            barrier,
            inc=1,
            device_id=(y * 2 + c, z * NX + x),
            device_id_type=pl.DeviceIdType.MESH,
        )
    pl.semaphore_wait(barrier, len(peers))


class Links:
    def __init__(self, y, c, z, x):
        self.at = (y, c, z, x)
        self.started = []

    def copy(self, src, dst, send_sem, recv_sem, y=None, c=None, z=None, x=None):
        here = self.at
        y, c, z, x = (own if new is None else new for new, own in zip((y, c, z, x), here))
        return pltpu.make_async_remote_copy(
            src_ref=src,
            dst_ref=dst,
            send_sem=send_sem,
            recv_sem=recv_sem,
            device_id=(y * 2 + c, z * NX + x),
            device_id_type=pl.DeviceIdType.MESH,
        )

    def send(self, src, dst, send_sem, recv_sem, **to):
        copy = self.copy(src, dst, send_sem, recv_sem, **to)
        copy.start()
        self.started.append(copy)

    def arrived(self, dst, send_sem, recv_sem):
        self.copy(dst, dst, send_sem, recv_sem).wait_recv()

    def finish(self):
        for copy in self.started:
            copy.wait_send()


def ring_gather(links, axis, count, me, view, half, send_sem, recv_sem):
    last = count // 2

    def got(way, step, part):
        links.arrived(
            half(view(-(1, -1)[way] * step, 0), part),
            send_sem.at[way, step, part],
            recv_sem.at[way, step, part],
        )

    for step in range(1, last + 1):
        new = []
        for part_at in range(2):
            for way, sign in enumerate((1, -1)):
                part = way if part_at == 0 else 1 - way
                k = -sign * (step - 1)
                if step > 1:
                    got(way, step - 1, part)
                    if part_at:
                        new.append(k)
                if step < last or part == way:
                    links.send(
                        half(view(k, 0), part), half(view(k, sign), part),
                        send_sem.at[way, step, part], recv_sem.at[way, step, part],
                        **{axis: wrap(me + sign, count)},
                    )
        if new:
            yield new
    for way in range(2):
        got(way, last, way)
    yield [last]


def ring_reduce(links, axis, count, me, own, sent, got, send_sem, recv_sem):
    last = count // 2
    for step in range(1, last + 1):
        yield step
        for part_at in range(2):
            for way, sign in enumerate((1, -1)):
                h = 1 - way if part_at == 0 else way
                if step == 1 and h != way:
                    continue
                value = own(sign * (last + 1 - step), h)
                if step > 2 or (step == 2 and h == way):
                    links.arrived(
                        got.at[way, step - 1, h],
                        send_sem.at[way, step - 1, h],
                        recv_sem.at[way, step - 1, h],
                    )
                    value = value + got[way, step - 1, h].astype(F32)
                sent[way, step, h] = value.astype(BF16)
                links.send(
                    sent.at[way, step, h], got.at[way, step, h],
                    send_sem.at[way, step, h], recv_sem.at[way, step, h],
                    **{axis: wrap(me + sign, count)},
                )
    yield last + 1
    for h in range(2):
        for way in range(2):
            links.arrived(
                got.at[way, last, h], send_sem.at[way, last, h], recv_sem.at[way, last, h]
            )


def drain(steps):
    for _ in steps:
        pass


def routing_table(routes, gates):
    lane = lax.broadcasted_iota(jnp.int32, (8, 128), 1)
    gate = jnp.zeros((8, 128), F32)
    named = jnp.zeros((8, 128), F32)
    for k in range(TOP):
        expert = routes[:, k : k + 1]
        gate = gate + jnp.where(expert == lane, gates[:, k : k + 1], 0.0)
        named = named + jnp.where(expert == lane - 32, 1.0, 0.0)
    row = lax.broadcasted_iota(jnp.int32, (8, 8), 0)
    col = lax.broadcasted_iota(jnp.int32, (8, 8), 1)
    before = jnp.dot((col < row).astype(F32), named, preferred_element_type=F32)
    return jnp.where(lane < 32, gate, jnp.where(named > 0.5, before, UNNAMED))


def matches(table, z):
    lane = lax.broadcasted_iota(jnp.int32, (128, 128), 1)
    row = lax.broadcasted_iota(jnp.int32, (128, NX * HALF), 1)
    token = lax.broadcasted_iota(jnp.int32, (128, NX * HALF), 0)
    slot = jnp.zeros((128, NX * HALF), F32)
    gate = jnp.zeros((128, NX * HALF), F32)
    for k in range(NX):
        expert = z * NX + k
        gate_col = jnp.sum(jnp.where(lane == expert, table, 0.0), axis=1, keepdims=True)
        slot_col = jnp.sum(jnp.where(lane == expert + 32, table, 0.0), axis=1, keepdims=True)
        mine = jnp.logical_and(row >= k * HALF, row < (k + 1) * HALF)
        slot = jnp.where(mine, slot_col, slot)
        gate = jnp.where(mine, gate_col, gate)
    inner = lax.rem(row, HALF)
    hit = jnp.logical_and(
        lax.div(token, 8) == lax.div(inner, CAP), slot == lax.rem(inner, CAP).astype(F32)
    )
    return jnp.where(hit, 1.0, 0.0).astype(BF16), jnp.where(hit, gate, 0.0).astype(BF16)


def attend(g, s, anc, live, q, lat, vup, keys):
    width = (ANC + 1) * BLK
    col = lax.broadcasted_iota(jnp.int32, (2 * BLK, width), 1)
    row = lax.rem(lax.broadcasted_iota(jnp.int32, (2 * BLK, width), 0), BLK)
    for a in range(ANC):
        keys[a * BLK : (a + 1) * BLK, :] = lat[jnp.maximum(anc[g, a], 0)]
    keys[ANC * BLK :, :] = lat[s * 4 + g]
    query = q[:, g * BLK : (g + 1) * BLK, :].reshape(2 * BLK, LAT + ROPE)
    scores = lax.dot_general(
        query, keys[...], (((1,), (1,)), ((), ())), preferred_element_type=F32
    ) * ((HD + ROPE) ** (-0.5))
    mask = jnp.logical_and(row >= col - ANC * BLK, live[g : g + 1, :] > 0.5)
    highest = jnp.max(jnp.where(mask, scores, MASKED), axis=1, keepdims=True)
    weights = jnp.where(mask, jnp.exp(scores - highest), 0.0)
    total = jnp.sum(weights, axis=1, keepdims=True)
    summed = jnp.dot(weights.astype(BF16), keys[:, :LAT], preferred_element_type=F32)
    latent = (summed / total).astype(BF16)
    return jnp.concatenate(
        [
            jnp.dot(latent[h * BLK : (h + 1) * BLK], vup[h], preferred_element_type=F32)
            for h in range(2)
        ],
        axis=1,
    ).astype(BF16)


def layer_kernel(
    anc, q_in, vup_in, gates_in, res_in, routes_in, anc_in, gain_in, lat_in, outp, wg, wu, wd,
    out,
    q, q_turned, vup, gates, res, routes, anc_rows, gain,
    lat, keys, meta, meta_all, res32, res_y, op_all, ho_a, ho_b, partial, a_sent, a_got,
    att, xrecv, hidden, squares, tokens, choose, combine, disp, rows, w_in, w_out,
    gsend, g_sent, g_got, act, dout, back, comb, c_sent, c_got, fin, orecv,
    loc, lat_s, lat_r, fwd_s, fwd_r, op_s, op_r, me_s, me_r, mz_s, mz_r, re_s, re_r,
    a1_s, a1_r, b1_s, b1_r, a2_s, a2_r, b2_s, b2_r, za_s, za_r, xa_s, xa_r, sq_s, sq_r,
    tk_s, tk_r, dp_s, dp_r, w_s, w_r, f_s, f_r, gy_s, gy_r, ac_s, ac_r, bk_s, bk_r,
    zc_s, zc_r, fo_s, fo_r,
):
    y, c, z, x = place()
    s = y * 2 + c
    other = 1 - c
    links = Links(y, c, z, x)
    send, arrived = links.send, links.arrived

    def weight_source(k, to):
        at = pl.ds(pl.multiple_of(to * DY, 128), DY)
        return (wg.at[at, :], wu.at[at, :], wd.at[:, at])[k]

    def weight_place(k, src):
        if k == 2:
            return w_out.at[pl.ds(pl.multiple_of(src * 128, 128), 128), :]
        return w_in.at[:, pl.ds(pl.multiple_of(k * FF + src * 128, 128), 128)]

    def send_weights(k, d):
        to = wrap(y + d, NY)
        send(weight_source(k, to), weight_place(k, s), w_s.at[k, d], w_r.at[k, d], y=to)

    def pass_on(k, d):
        block = weight_place(k, wrap(y - d, NY) * 2 + c)
        arrived(block, w_s.at[k, d], w_r.at[k, d])
        send(block, block, f_s.at[k, d], f_r.at[k, d], c=other)

    def from_other(k):
        own[2 + k].wait()
        for d in range(NY):
            block = weight_place(k, wrap(y - d, NY) * 2 + other)
            arrived(block, f_s.at[k, d], f_r.at[k, d])

    def op_columns(to):
        start = pl.multiple_of(y * DY + jnp.minimum(to * CW, DY - CW), 128)
        return outp.at[:, pl.ds(start, CW)]

    own = [
        pltpu.make_async_copy(lat_in, lat.at[pl.ds(s * 4, 4)], loc.at[0]),
        pltpu.make_async_copy(op_columns(x), op_all.at[x], loc.at[1]),
    ] + [
        pltpu.make_async_copy(weight_source(k, y), weight_place(k, s), loc.at[2 + k])
        for k in range(3)
    ]
    small = [
        pltpu.make_async_copy(src, dst, loc.at[5 + k])
        for k, (src, dst) in enumerate(
            (
                (routes_in, routes),
                (gates_in, gates),
                (res_in, res),
                (anc_in, anc_rows),
                (gain_in, gain),
                (q_in, q_turned),
                (vup_in, vup),
            )
        )
    ]
    for copy in own[:1] + small + own[1:]:
        copy.start()
    for copy in small[:3]:
        copy.wait()
    meta[...] = routing_table(routes[...], gates[...])
    meta_all[1, y] = meta[...]
    res32[...] = res[...].astype(F32)
    meet(
        [(wrap(y + d, NY), c, z, x) for d in range(1, NY)]
        + [(y, c, wrap(z + d, NZ), x) for d in range(1, NZ)]
        + [(y, c, z, wrap(x + d, NX)) for d in range(1, NX)]
        + [(y, other, z, x)]
    )

    own[0].wait()

    def lat_view(k, shift):
        return lat.at[pl.ds((wrap(y + k, NY) * 2 + c) * 4, 4)]

    lat_ring = ring_gather(
        links, "y", NY, y, lat_view, lambda ref, h: ref.at[pl.ds(h * 2, 2)], lat_s, lat_r
    )

    def forward(k):
        block = lat_view(k, 0)
        send(block, block, fwd_s.at[k % NY], fwd_r.at[k % NY], c=other)

    for d in range(1, NY):
        to = wrap(y + d, NY)
        send(meta, meta_all.at[1, y], me_s.at[d], me_r.at[d], y=to)
    first = next(lat_ring)
    forward(0)
    for k in first:
        forward(k)
    for k in range(2):
        for d in (1, 3):
            send_weights(k, d)
    for d in range(1, NX):
        to = wrap(x + d, NX)
        send(op_columns(to), op_all.at[x], op_s.at[d], op_r.at[d], x=to)
    for d in range(1, NY):
        arrived(meta_all.at[1, wrap(y - d, NY)], me_s.at[d], me_r.at[d])
    for d in range(1, NZ):
        send(meta_all.at[1], meta_all.at[(d + 1) % NZ], mz_s.at[d], mz_r.at[d], z=wrap(z + d, NZ))
    res_y[y] = res32[:, pl.ds(pl.multiple_of(y * DY, 128), DY)]
    for copy in small[3:]:
        copy.wait()
    for h in range(2):
        q[h] = q_turned[h].T
    area = lax.broadcasted_iota(jnp.int32, (ANC, (ANC + 1) * BLK), 1)
    slot_of = lax.broadcasted_iota(jnp.int32, (ANC, (ANC + 1) * BLK), 0)
    spread = (lax.div(area, BLK) == slot_of).astype(F32)
    live = jnp.dot((anc_rows[...] >= 0).astype(F32), spread, preferred_element_type=F32) + (
        lax.broadcasted_iota(jnp.int32, (4, (ANC + 1) * BLK), 1) >= ANC * BLK
    ).astype(F32)
    for new in lat_ring:
        for k in new:
            forward(k)
    for k in range(3):
        send(
            weight_source(k, y), weight_place(k, s), f_s.at[k, 0], f_r.at[k, 0], c=other
        )
    for k in range(NY):
        block = lat.at[pl.ds((wrap(y + k, NY) * 2 + other) * 4, 4)]
        arrived(block, fwd_s.at[k], fwd_r.at[k])

    for g in range(2):
        ho_a[y, x, g * BLK : (g + 1) * BLK, :] = attend(g, s, anc, live, q, lat, vup, keys)
    for d in range(1, NX):
        send(ho_a.at[y, x], ho_a.at[y, x], a1_s.at[d], a1_r.at[d], x=wrap(x + d, NX))
    for g in range(2):
        ho_b[x, y, g * BLK : (g + 1) * BLK, :] = attend(g + 2, s, anc, live, q, lat, vup, keys)
    for d in range(1, NY):
        send(ho_b.at[x, y], ho_b.at[x, y], b1_s.at[d], b1_r.at[d], y=wrap(y + d, NY))

    def pairs(ref, h):
        return ref.at[pl.ds(h * 2, 2)]

    a_ring = ring_gather(
        links, "y", NY, y, lambda k, shift: ho_a.at[wrap(y + k, NY)], pairs, a2_s, a2_r
    )
    b_ring = ring_gather(
        links, "x", NX, x, lambda k, shift: ho_b.at[wrap(x + k, NX)], pairs, b2_s, b2_r
    )
    for d in range(1, NX):
        arrived(ho_a.at[y, wrap(x - d, NX)], a1_s.at[d], a1_r.at[d])
    for d in range(1, NY):
        arrived(ho_b.at[x, wrap(y - d, NY)], b1_s.at[d], b1_r.at[d])
    next(a_ring)
    next(b_ring)
    for d in range(1, NZ):
        arrived(meta_all.at[(d + 1) % NZ], mz_s.at[d], mz_r.at[d])
    for h in range(2):
        pick, weigh = matches(meta_all[4 * h : 4 * h + 4].reshape(128, 128), z)
        choose[h] = pick
        combine[h] = weigh
    for d in range(1, NX):
        arrived(op_all.at[wrap(x - d, NX)], op_s.at[d], op_r.at[d])
    own[1].wait()
    drain(a_ring)
    drain(b_ring)
    for d in range(1, NY):
        to = wrap(y + d, NY)
        part = res32.at[:, pl.ds(pl.multiple_of(to * DY, 128), DY)]
        send(part, res_y.at[y], re_s.at[d], re_r.at[d], y=to)
    send_weights(0, 2)
    send_weights(1, 2)
    for k in range(2):
        for d in (1, 3):
            pass_on(k, d)

    for n in range(NY):
        for low, block in ((0, lambda k: ho_a[n, k]), (4, lambda k: ho_b[k, n])):
            total = None
            for k in range(NX):
                part = jnp.dot(block(k), op_all[k], preferred_element_type=F32)
                total = part if total is None else total + part
            total = total.astype(BF16)
            for k in range(4):
                partial[low + k, n] = total[k * 32 : (k + 1) * 32]

    def attention_term(k, h):
        return partial[wrap(z + k, NZ), 2 * h : 2 * h + 2].astype(F32)

    drain(ring_reduce(links, "z", NZ, z, attention_term, a_sent, a_got, za_s, za_r))
    for h in range(2):
        total = (
            attention_term(0, h)
            + a_got[0, NZ // 2, h].astype(F32)
            + a_got[1, NZ // 2, h].astype(F32)
        )
        for k in range(NX):
            att[k, 2 * h : 2 * h + 2] = total[:, k * 8 : (k + 1) * 8]
    for d in range(1, NX):
        to = wrap(x + d, NX)
        send(att.at[to], xrecv.at[x], xa_s.at[d], xa_r.at[d], x=to)
    xrecv[x] = att[x]
    for d in range(1, NY):
        arrived(res_y.at[wrap(y - d, NY)], re_s.at[d], re_r.at[d])
    for d in range(1, NX):
        arrived(xrecv.at[wrap(x - d, NX)], xa_s.at[d], xa_r.at[d])
    for k in range(NX):
        low = NX * CW - DY if k == NX - 1 else 0
        at, wide = k * CW, CW - low
        hidden[:, at : at + wide] = xrecv[k].reshape(NY * 8, CW)[:, low:] + res_y[
            :, :, at : at + wide
        ].reshape(NY * 8, wide)
    held = hidden[...]
    squares[y] = jnp.broadcast_to(jnp.sum(held * held, axis=1, keepdims=True), (NY * 8, 128))
    for d in range(1, NY):
        send(squares.at[y], squares.at[y], sq_s.at[d], sq_r.at[d], y=wrap(y + d, NY))
    for d in range(1, NY):
        arrived(squares.at[wrap(y - d, NY)], sq_s.at[d], sq_r.at[d])
    for d in (1, 3, 2):
        send_weights(2, d)
    mean = (squares[0] + squares[1] + squares[2] + squares[3])[:, :1] * (1.0 / D)
    tokens[1] = (held * lax.rsqrt(mean + NORM_EPS) * gain[pl.ds(pl.multiple_of(y * DY, 256), DY)].astype(F32).reshape(1, DY)).astype(BF16)
    token_ring = ring_gather(
        links, "z", NZ, z,
        lambda k, shift: tokens.at[(1 - k + shift) % NZ],
        lambda ref, h: ref.at[pl.ds(h * 16, 16)],
        tk_s, tk_r,
    )

    def dispatch(h):
        table = tokens[4 * h : 4 * h + 4].reshape(128, DY)
        chosen = lax.dot_general(
            choose[h], table, (((0,), (0,)), ((), ())), preferred_element_type=F32
        ).astype(BF16)
        for k in range(NX):
            disp[h, k] = chosen[k * HALF : (k + 1) * HALF]
        for d in (2, 1, 3):
            to = wrap(x + d, NX)
            send(disp.at[h, to], rows.at[x, h], dp_s.at[h, d], dp_r.at[h, d], x=to)
        rows[x, h] = disp[h, x]

    next(token_ring)
    next(token_ring)
    dispatch(0)
    next(token_ring)
    for k in range(2):
        pass_on(k, 2)
    drain(token_ring)
    dispatch(1)
    for k in range(2):
        from_other(k)
    for d in (1, 3, 2):
        pass_on(2, d)

    def enter(h):
        for d in range(1, NX):
            arrived(rows.at[wrap(x - d, NX), h], dp_s.at[h, d], dp_r.at[h, d])

        def inward(j, _):
            at = pl.ds(pl.multiple_of(j * 512, 512), 512)
            part = jnp.dot(
                rows[:, h].reshape(NX * HALF, DY), w_in[:, at], preferred_element_type=F32
            ).astype(BF16)
            for k in range(NX):
                gsend[k, h, :, at] = part[k * HALF : (k + 1) * HALF]
            return 0

        lax.fori_loop(0, 2 * FF // 512, inward, 0)

    def inward_term(h):
        return lambda k, part: gsend[
            wrap(y + k, NY), h, :, part * FF : (part + 1) * FF
        ].astype(F32)

    def sum_ring(h):
        return ring_reduce(
            links, "y", NY, y, inward_term(h), g_sent.at[h], g_got.at[h], gy_s.at[h], gy_r.at[h]
        )

    def activate(h):
        gate, up = (
            inward_term(h)(0, part)
            + g_got[h, 0, NY // 2, part].astype(F32)
            + g_got[h, 1, NY // 2, part].astype(F32)
            for part in range(2)
        )
        act[y, h] = (gate / (1.0 + jnp.exp(-gate)) * up).astype(BF16)

    def act_ring(h):
        return ring_gather(
            links, "y", NY, y, lambda k, shift: act.at[wrap(y + k, NY), h],
            lambda ref, part: ref.at[:, pl.ds(part * (FF // 2), FF // 2)],
            ac_s.at[h], ac_r.at[h],
        )

    def leave(h):
        def outward(j, _):
            at = pl.ds(pl.multiple_of(j * 256, 256), 256)
            part = jnp.dot(
                act[:, h].reshape(NX * HALF, FF), w_out[:, at], preferred_element_type=F32
            ).astype(BF16)
            for k in range(NX):
                dout[h, k, :, at] = part[k * HALF : (k + 1) * HALF]
            return 0

        lax.fori_loop(0, DY // 256, outward, 0)
        for d in (2, 1, 3):
            to = wrap(x + d, NX)
            send(dout.at[h, to], back.at[h, x], bk_s.at[h, d], bk_r.at[h, d], x=to)
        back[h, x] = dout[h, x]

    sums = [sum_ring(0), sum_ring(1)]
    acts = [act_ring(0), act_ring(1)]
    enter(0)
    for _ in range(3):
        next(sums[0])
    enter(1)
    next(sums[1])
    next(sums[1])
    drain(sums[0])
    activate(0)
    next(acts[0])
    next(acts[0])
    next(sums[1])
    drain(acts[0])
    from_other(2)
    drain(sums[1])
    activate(1)
    next(acts[1])
    leave(0)
    drain(acts[1])
    leave(1)

    def weigh_rows(h):
        for d in range(1, NX):
            arrived(back.at[h, wrap(x - d, NX)], bk_s.at[h, d], bk_r.at[h, d])

        def gather(j, _):
            at = pl.ds(pl.multiple_of(j * 256, 256), 256)
            part = jnp.dot(
                combine[h], back[h, :, :, at].reshape(NX * HALF, 256), preferred_element_type=F32
            )
            for k in range(4):
                comb[4 * h + k, :, at] = part[k * 32 : (k + 1) * 32]
            return 0

        lax.fori_loop(0, DY // 256, gather, 0)

    def token_term(k, h):
        return comb[(1 - k) % NZ, h * 16 : (h + 1) * 16]

    weigh_rows(0)
    weigh_rows(1)
    drain(ring_reduce(links, "z", NZ, z, token_term, c_sent, c_got, zc_s, zc_r))
    for h in range(2):
        total = (
            hidden[h * 16 : (h + 1) * 16]
            + token_term(0, h)
            + c_got[0, NZ // 2, h].astype(F32)
            + c_got[1, NZ // 2, h].astype(F32)
        )
        fin[2 * h] = total[:8]
        fin[2 * h + 1] = total[8:]
    for d in (2, 1, 3):
        to = wrap(y + d, NY)
        send(fin.at[to], orecv.at[y], fo_s.at[d], fo_r.at[d], y=to)
    orecv[y] = fin[y]
    for d in range(1, NY):
        arrived(orecv.at[wrap(y - d, NY)], fo_s.at[d], fo_r.at[d])
    for k in range(NY):
        out[:, k * DY : (k + 1) * DY] = orecv[k]
    links.finish()


def layer(*operands):
    def two(*shape):
        return [DMA(shape), DMA(shape)]

    return pl.pallas_call(
        layer_kernel,
        out_shape=jax.ShapeDtypeStruct((8, D), F32),
        in_specs=[SMEM] + [ANY] * 12,
        out_specs=VMEM,
        scratch_shapes=[
            pltpu.VMEM((2, 256, LAT + ROPE), BF16),
            pltpu.VMEM((2, LAT + ROPE, 256), BF16),
            pltpu.VMEM((2, LAT, HD), BF16),
            pltpu.VMEM((8, TOP), F32),
            pltpu.VMEM((8, D), BF16),
            pltpu.VMEM((8, TOP), jnp.int32),
            pltpu.VMEM((4, ANC), jnp.int32),
            pltpu.VMEM((D,), BF16),
            pltpu.VMEM((32, BLK, LAT + ROPE), BF16),
            pltpu.VMEM(((ANC + 1) * BLK, LAT + ROPE), BF16),
            pltpu.VMEM((8, 128), F32),
            pltpu.VMEM((NZ, NY, 8, 128), F32),
            pltpu.VMEM((8, D), F32),
            pltpu.VMEM((NY, 8, DY), F32),
            pltpu.VMEM((NX, 256, CW), BF16),
            pltpu.VMEM((NY, NX, 128, 256), BF16),
            pltpu.VMEM((NX, NY, 128, 256), BF16),
            pltpu.VMEM((NZ, NY, 32, CW), BF16),
            pltpu.VMEM((2, NZ // 2 + 1, 2, 2, 32, CW), BF16),
            pltpu.VMEM((2, NZ // 2 + 1, 2, 2, 32, CW), BF16),
            pltpu.VMEM((NX, NY, 8, CW), F32),
            pltpu.VMEM((NX, NY, 8, CW), F32),
            pltpu.VMEM((NY * 8, DY), F32),
            pltpu.VMEM((NY, NY * 8, 128), F32),
            pltpu.VMEM((NZ, NY * 8, DY), BF16),
            pltpu.VMEM((2, 128, NX * HALF), BF16),
            pltpu.VMEM((2, 128, NX * HALF), BF16),
            pltpu.VMEM((2, NX, HALF, DY), BF16),
            pltpu.VMEM((NX, 2, HALF, DY), BF16),
            pltpu.VMEM((DY, 2 * FF), BF16),
            pltpu.VMEM((FF, DY), BF16),
            pltpu.VMEM((NY, 2, HALF, 2 * FF), BF16),
            pltpu.VMEM((2, 2, NY // 2 + 1, 2, HALF, FF), BF16),
            pltpu.VMEM((2, 2, NY // 2 + 1, 2, HALF, FF), BF16),
            pltpu.VMEM((NY, 2, HALF, FF), BF16),
            pltpu.VMEM((2, NX, HALF, DY), BF16),
            pltpu.VMEM((2, NX, HALF, DY), BF16),
            pltpu.VMEM((NZ, NY * 8, DY), F32),
            pltpu.VMEM((2, NZ // 2 + 1, 2, 16, DY), BF16),
            pltpu.VMEM((2, NZ // 2 + 1, 2, 16, DY), BF16),
            pltpu.VMEM((NY, 8, DY), F32),
            pltpu.VMEM((NY, 8, DY), F32),
            DMA((12,)),
            *two(2, NY // 2 + 1, 2),
            *two(NY),
            *two(NX),
            *two(NY),
            *two(NZ),
            *two(NY),
            *two(NX),
            *two(NY),
            *two(2, NY // 2 + 1, 2),
            *two(2, NX // 2 + 1, 2),
            *two(2, NZ // 2 + 1, 2),
            *two(NX),
            *two(NY),
            *two(2, NZ // 2 + 1, 2),
            *two(2, NX),
            *two(3, NY),
            *two(3, NY),
            *two(2, 2, NY // 2 + 1, 2),
            *two(2, 2, NY // 2 + 1, 2),
            *two(2, NX),
            *two(2, NZ // 2 + 1, 2),
            *two(NY),
        ],
        compiler_params=pltpu.CompilerParams(
            collective_id=0, has_side_effects=True, vmem_limit_bytes=63 << 20
        ),
        name="layer",
    )(*operands)


def on_device(
    queries,
    latent_cache,
    ancestors,
    value_up,
    out_proj,
    residual,
    norm_gain,
    routes,
    gates,
    w_gate,
    w_up,
    w_down,
):
    final = layer(
        ancestors,
        queries.transpose(1, 2, 0),
        value_up,
        gates,
        residual,
        routes,
        ancestors,
        norm_gain,
        latent_cache,
        out_proj,
        w_gate[0],
        w_up[0],
        w_down[0],
    )
    return final.astype(BF16)


def solution(mesh):
    placed = (
        P("seq", "exp", None),
        P("seq", None, None),
        P("seq", None),
        P("exp", None, None),
        P("exp", None),
        P(("seq", "exp"), None),
        P(),
        P(("seq", "exp"), None),
        P(("seq", "exp"), None),
        P("exp", None, "seq"),
        P("exp", None, "seq"),
        P("exp", "seq", None),
    )
    return jax.shard_map(
        on_device, mesh=mesh, in_specs=placed, out_specs=P(("seq", "exp"), None), check_vma=False
    )
```

```python
import jax
import jax.numpy as jnp
from jax import lax
from jax.experimental import pallas as pl
from jax.experimental.pallas import tpu as pltpu
from jax.sharding import PartitionSpec as P

D = 7168
LAT = 512
ROPE = 64
HD = 128
BLK = 64
ANC = 8
TOP = 8
CAP = 3
NY, NZ, NX = 4, 8, 4
DY = D // NY
CW = 512
FF = 1024
HALF = 48
UNNAMED = 99.0
NORM_EPS = 1e-6
MASKED = -1e30
F32 = jnp.float32
BF16 = jnp.bfloat16
ANY = pl.BlockSpec(memory_space=pl.ANY)
VMEM = pl.BlockSpec(memory_space=pltpu.VMEM)
SMEM = pl.BlockSpec(memory_space=pltpu.SMEM)
DMA = pltpu.SemaphoreType.DMA


def place():
    s = lax.axis_index("seq")
    e = lax.axis_index("exp")
    return lax.div(s, 2), lax.rem(s, 2), lax.div(e, NX), lax.rem(e, NX)


def wrap(value, count):
    return lax.rem(value + count, count)


def meet(peers):
    barrier = pltpu.get_barrier_semaphore()
    for y, c, z, x in peers:
        pl.semaphore_signal(
            barrier,
            inc=1,
            device_id=(y * 2 + c, z * NX + x),
            device_id_type=pl.DeviceIdType.MESH,
        )
    pl.semaphore_wait(barrier, len(peers))


class Links:
    def __init__(self, y, c, z, x):
        self.at = (y, c, z, x)
        self.started = []

    def copy(self, src, dst, send_sem, recv_sem, y=None, c=None, z=None, x=None):
        here = self.at
        y, c, z, x = (own if new is None else new for new, own in zip((y, c, z, x), here))
        return pltpu.make_async_remote_copy(
            src_ref=src,
            dst_ref=dst,
            send_sem=send_sem,
            recv_sem=recv_sem,
            device_id=(y * 2 + c, z * NX + x),
            device_id_type=pl.DeviceIdType.MESH,
        )

    def send(self, src, dst, send_sem, recv_sem, **to):
        copy = self.copy(src, dst, send_sem, recv_sem, **to)
        copy.start()
        self.started.append(copy)

    def arrived(self, dst, send_sem, recv_sem):
        self.copy(dst, dst, send_sem, recv_sem).wait_recv()

    def finish(self):
        for copy in self.started:
            copy.wait_send()


def ring_gather(links, axis, count, me, view, half, send_sem, recv_sem):
    last = count // 2

    def got(way, step, part):
        links.arrived(
            half(view(-(1, -1)[way] * step, 0), part),
            send_sem.at[way, step, part],
            recv_sem.at[way, step, part],
        )

    for step in range(1, last + 1):
        new = []
        for part_at in range(2):
            for way, sign in enumerate((1, -1)):
                part = way if part_at == 0 else 1 - way
                k = -sign * (step - 1)
                if step > 1:
                    got(way, step - 1, part)
                    if part_at:
                        new.append(k)
                if step < last or part == way:
                    links.send(
                        half(view(k, 0), part), half(view(k, sign), part),
                        send_sem.at[way, step, part], recv_sem.at[way, step, part],
                        **{axis: wrap(me + sign, count)},
                    )
        if new:
            yield new
    for way in range(2):
        got(way, last, way)
    yield [last]


def ring_reduce(links, axis, count, me, own, sent, got, send_sem, recv_sem):
    last = count // 2
    for step in range(1, last + 1):
        yield step
        for part_at in range(2):
            for way, sign in enumerate((1, -1)):
                h = 1 - way if part_at == 0 else way
                if step == 1 and h != way:
                    continue
                value = own(sign * (last + 1 - step), h)
                if step > 2 or (step == 2 and h == way):
                    links.arrived(
                        got.at[way, step - 1, h],
                        send_sem.at[way, step - 1, h],
                        recv_sem.at[way, step - 1, h],
                    )
                    value = value + got[way, step - 1, h].astype(F32)
                sent[way, step, h] = value.astype(BF16)
                links.send(
                    sent.at[way, step, h], got.at[way, step, h],
                    send_sem.at[way, step, h], recv_sem.at[way, step, h],
                    **{axis: wrap(me + sign, count)},
                )
    yield last + 1
    for h in range(2):
        for way in range(2):
            links.arrived(
                got.at[way, last, h], send_sem.at[way, last, h], recv_sem.at[way, last, h]
            )


def drain(steps):
    for _ in steps:
        pass


def routing_table(routes, gates):
    lane = lax.broadcasted_iota(jnp.int32, (8, 128), 1)
    gate = jnp.zeros((8, 128), F32)
    named = jnp.zeros((8, 128), F32)
    for k in range(TOP):
        expert = routes[:, k : k + 1]
        gate = gate + jnp.where(expert == lane, gates[:, k : k + 1], 0.0)
        named = named + jnp.where(expert == lane - 32, 1.0, 0.0)
    row = lax.broadcasted_iota(jnp.int32, (8, 8), 0)
    col = lax.broadcasted_iota(jnp.int32, (8, 8), 1)
    before = jnp.dot((col < row).astype(F32), named, preferred_element_type=F32)
    return jnp.where(lane < 32, gate, jnp.where(named > 0.5, before, UNNAMED))


def matches(table, z):
    lane = lax.broadcasted_iota(jnp.int32, (128, 128), 1)
    row = lax.broadcasted_iota(jnp.int32, (128, NX * HALF), 1)
    token = lax.broadcasted_iota(jnp.int32, (128, NX * HALF), 0)
    slot = jnp.zeros((128, NX * HALF), F32)
    gate = jnp.zeros((128, NX * HALF), F32)
    for k in range(NX):
        expert = z * NX + k
        gate_col = jnp.sum(jnp.where(lane == expert, table, 0.0), axis=1, keepdims=True)
        slot_col = jnp.sum(jnp.where(lane == expert + 32, table, 0.0), axis=1, keepdims=True)
        mine = jnp.logical_and(row >= k * HALF, row < (k + 1) * HALF)
        slot = jnp.where(mine, slot_col, slot)
        gate = jnp.where(mine, gate_col, gate)
    inner = lax.rem(row, HALF)
    hit = jnp.logical_and(
        lax.div(token, 8) == lax.div(inner, CAP), slot == lax.rem(inner, CAP).astype(F32)
    )
    return jnp.where(hit, 1.0, 0.0).astype(BF16), jnp.where(hit, gate, 0.0).astype(BF16)


def attend(g, s, anc, live, q, lat, vup, keys):
    width = (ANC + 1) * BLK
    col = lax.broadcasted_iota(jnp.int32, (2 * BLK, width), 1)
    row = lax.rem(lax.broadcasted_iota(jnp.int32, (2 * BLK, width), 0), BLK)
    for a in range(ANC):
        keys[a * BLK : (a + 1) * BLK, :] = lat[jnp.maximum(anc[g, a], 0)]
    keys[ANC * BLK :, :] = lat[s * 4 + g]
    query = q[:, g * BLK : (g + 1) * BLK, :].reshape(2 * BLK, LAT + ROPE)
    scores = lax.dot_general(
        query, keys[...], (((1,), (1,)), ((), ())), preferred_element_type=F32
    ) * ((HD + ROPE) ** (-0.5))
    mask = jnp.logical_and(row >= col - ANC * BLK, live[g : g + 1, :] > 0.5)
    highest = jnp.max(jnp.where(mask, scores, MASKED), axis=1, keepdims=True)
    weights = jnp.where(mask, jnp.exp(scores - highest), 0.0)
    total = jnp.sum(weights, axis=1, keepdims=True)
    summed = jnp.dot(weights.astype(BF16), keys[:, :LAT], preferred_element_type=F32)
    latent = (summed / total).astype(BF16)
    return jnp.concatenate(
        [
            jnp.dot(latent[h * BLK : (h + 1) * BLK], vup[h], preferred_element_type=F32)
            for h in range(2)
        ],
        axis=1,
    ).astype(BF16)


def layer_kernel(
    anc, q_in, vup_in, gates_in, res_in, routes_in, anc_in, gain_in, lat_in, outp, wg, wu, wd,
    out,
    q, q_turned, vup, gates, res, routes, anc_rows, gain,
    lat, keys, meta, meta_all, res32, res_y, op_all, ho_a, ho_b, partial, a_sent, a_got,
    att, xrecv, hidden, squares, tokens, choose, combine, disp, rows, w_in, w_out,
    gsend, g_sent, g_got, act, dout, back, comb, c_sent, c_got, fin, orecv,
    loc, lat_s, lat_r, fwd_s, fwd_r, op_s, op_r, me_s, me_r, mz_s, mz_r, re_s, re_r,
    a1_s, a1_r, b1_s, b1_r, a2_s, a2_r, b2_s, b2_r, za_s, za_r, xa_s, xa_r, sq_s, sq_r,
    tk_s, tk_r, dp_s, dp_r, w_s, w_r, f_s, f_r, gy_s, gy_r, ac_s, ac_r, bk_s, bk_r,
    zc_s, zc_r, fo_s, fo_r,
):
    y, c, z, x = place()
    s = y * 2 + c
    other = 1 - c
    links = Links(y, c, z, x)
    send, arrived = links.send, links.arrived

    def weight_source(k, to):
        at = pl.ds(pl.multiple_of(to * DY, 128), DY)
        return (wg.at[at, :], wu.at[at, :], wd.at[:, at])[k]

    def weight_place(k, src):
        if k == 2:
            return w_out.at[pl.ds(pl.multiple_of(src * 128, 128), 128), :]
        return w_in.at[:, pl.ds(pl.multiple_of(k * FF + src * 128, 128), 128)]

    def send_weights(k, d):
        to = wrap(y + d, NY)
        send(weight_source(k, to), weight_place(k, s), w_s.at[k, d], w_r.at[k, d], y=to)

    def pass_on(k, d):
        block = weight_place(k, wrap(y - d, NY) * 2 + c)
        arrived(block, w_s.at[k, d], w_r.at[k, d])
        send(block, block, f_s.at[k, d], f_r.at[k, d], c=other)

    def from_other(k):
        own[2 + k].wait()
        for d in range(NY):
            block = weight_place(k, wrap(y - d, NY) * 2 + other)
            arrived(block, f_s.at[k, d], f_r.at[k, d])

    def op_columns(to):
        start = pl.multiple_of(y * DY + jnp.minimum(to * CW, DY - CW), 128)
        return outp.at[:, pl.ds(start, CW)]

    own = [
        pltpu.make_async_copy(lat_in, lat.at[pl.ds(s * 4, 4)], loc.at[0]),
        pltpu.make_async_copy(op_columns(x), op_all.at[x], loc.at[1]),
    ] + [
        pltpu.make_async_copy(weight_source(k, y), weight_place(k, s), loc.at[2 + k])
        for k in range(3)
    ]
    small = [
        pltpu.make_async_copy(src, dst, loc.at[5 + k])
        for k, (src, dst) in enumerate(
            (
                (routes_in, routes),
                (gates_in, gates),
                (res_in, res),
                (anc_in, anc_rows),
                (gain_in, gain),
                (q_in, q_turned),
                (vup_in, vup),
            )
        )
    ]
    for copy in own[:1] + small + own[1:]:
        copy.start()
    for copy in small[:3]:
        copy.wait()
    meta[...] = routing_table(routes[...], gates[...])
    meta_all[1, y] = meta[...]
    res32[...] = res[...].astype(F32)
    meet(
        [(wrap(y + d, NY), c, z, x) for d in range(1, NY)]
        + [(y, c, wrap(z + d, NZ), x) for d in range(1, NZ)]
        + [(y, c, z, wrap(x + d, NX)) for d in range(1, NX)]
        + [(y, other, z, x)]
    )

    own[0].wait()

    def lat_view(k, shift):
        return lat.at[pl.ds((wrap(y + k, NY) * 2 + c) * 4, 4)]

    lat_ring = ring_gather(
        links, "y", NY, y, lat_view, lambda ref, h: ref.at[pl.ds(h * 2, 2)], lat_s, lat_r
    )

    def forward(k):
        block = lat_view(k, 0)
        send(block, block, fwd_s.at[k % NY], fwd_r.at[k % NY], c=other)

    for d in range(1, NY):
        to = wrap(y + d, NY)
        send(meta, meta_all.at[1, y], me_s.at[d], me_r.at[d], y=to)
    first = next(lat_ring)
    forward(0)
    for k in first:
        forward(k)
    for k in range(2):
        for d in (1, 3):
            send_weights(k, d)
    for d in range(1, NX):
        to = wrap(x + d, NX)
        send(op_columns(to), op_all.at[x], op_s.at[d], op_r.at[d], x=to)
    for d in range(1, NY):
        arrived(meta_all.at[1, wrap(y - d, NY)], me_s.at[d], me_r.at[d])
    for d in range(1, NZ):
        send(meta_all.at[1], meta_all.at[(d + 1) % NZ], mz_s.at[d], mz_r.at[d], z=wrap(z + d, NZ))
    res_y[y] = res32[:, pl.ds(pl.multiple_of(y * DY, 128), DY)]
    for copy in small[3:]:
        copy.wait()
    for h in range(2):
        q[h] = q_turned[h].T
    area = lax.broadcasted_iota(jnp.int32, (ANC, (ANC + 1) * BLK), 1)
    slot_of = lax.broadcasted_iota(jnp.int32, (ANC, (ANC + 1) * BLK), 0)
    spread = (lax.div(area, BLK) == slot_of).astype(F32)
    live = jnp.dot((anc_rows[...] >= 0).astype(F32), spread, preferred_element_type=F32) + (
        lax.broadcasted_iota(jnp.int32, (4, (ANC + 1) * BLK), 1) >= ANC * BLK
    ).astype(F32)
    for new in lat_ring:
        for k in new:
            forward(k)
    for k in range(3):
        send(
            weight_source(k, y), weight_place(k, s), f_s.at[k, 0], f_r.at[k, 0], c=other
        )
    for k in range(NY):
        block = lat.at[pl.ds((wrap(y + k, NY) * 2 + other) * 4, 4)]
        arrived(block, fwd_s.at[k], fwd_r.at[k])

    for g in range(2):
        ho_a[y, x, g * BLK : (g + 1) * BLK, :] = attend(g, s, anc, live, q, lat, vup, keys)
    for d in range(1, NX):
        send(ho_a.at[y, x], ho_a.at[y, x], a1_s.at[d], a1_r.at[d], x=wrap(x + d, NX))
    for g in range(2):
        ho_b[x, y, g * BLK : (g + 1) * BLK, :] = attend(g + 2, s, anc, live, q, lat, vup, keys)
    for d in range(1, NY):
        send(ho_b.at[x, y], ho_b.at[x, y], b1_s.at[d], b1_r.at[d], y=wrap(y + d, NY))

    def pairs(ref, h):
        return ref.at[pl.ds(h * 2, 2)]

    a_ring = ring_gather(
        links, "y", NY, y, lambda k, shift: ho_a.at[wrap(y + k, NY)], pairs, a2_s, a2_r
    )
    b_ring = ring_gather(
        links, "x", NX, x, lambda k, shift: ho_b.at[wrap(x + k, NX)], pairs, b2_s, b2_r
    )
    for d in range(1, NX):
        arrived(ho_a.at[y, wrap(x - d, NX)], a1_s.at[d], a1_r.at[d])
    for d in range(1, NY):
        arrived(ho_b.at[x, wrap(y - d, NY)], b1_s.at[d], b1_r.at[d])
    next(a_ring)
    next(b_ring)
    for d in range(1, NZ):
        arrived(meta_all.at[(d + 1) % NZ], mz_s.at[d], mz_r.at[d])
    for h in range(2):
        pick, weigh = matches(meta_all[4 * h : 4 * h + 4].reshape(128, 128), z)
        choose[h] = pick.T
        combine[h] = weigh
    for d in range(1, NX):
        arrived(op_all.at[wrap(x - d, NX)], op_s.at[d], op_r.at[d])
    own[1].wait()
    drain(a_ring)
    drain(b_ring)
    for d in range(1, NY):
        to = wrap(y + d, NY)
        part = res32.at[:, pl.ds(pl.multiple_of(to * DY, 128), DY)]
        send(part, res_y.at[y], re_s.at[d], re_r.at[d], y=to)
    send_weights(0, 2)
    send_weights(1, 2)
    for k in range(2):
        for d in (1, 3):
            pass_on(k, d)

    for n in range(NY):
        for low, block in ((0, lambda k: ho_a[n, k]), (4, lambda k: ho_b[k, n])):
            total = None
            for k in range(NX):
                part = jnp.dot(block(k), op_all[k], preferred_element_type=F32)
                total = part if total is None else total + part
            total = total.astype(BF16)
            for k in range(4):
                partial[low + k, n] = total[k * 32 : (k + 1) * 32]

    def attention_term(k, h):
        return partial[wrap(z + k, NZ), 2 * h : 2 * h + 2].astype(F32)

    drain(ring_reduce(links, "z", NZ, z, attention_term, a_sent, a_got, za_s, za_r))
    summed = jnp.concatenate(
        [
            attention_term(0, h)
            + a_got[0, NZ // 2, h].astype(F32)
            + a_got[1, NZ // 2, h].astype(F32)
            for h in range(2)
        ],
        axis=0,
    )
    for k in range(NX):
        att[k] = summed[:, k * 8 : (k + 1) * 8].reshape(NY * 8, CW).astype(BF16)
    for d in range(1, NX):
        to = wrap(x + d, NX)
        send(att.at[to], xrecv.at[x], xa_s.at[d], xa_r.at[d], x=to)
    xrecv[x] = att[x]
    for d in range(1, NY):
        arrived(res_y.at[wrap(y - d, NY)], re_s.at[d], re_r.at[d])
    for d in range(1, NX):
        arrived(xrecv.at[wrap(x - d, NX)], xa_s.at[d], xa_r.at[d])
    for k in range(NX):
        low = NX * CW - DY if k == NX - 1 else 0
        at, wide = k * CW, CW - low
        hidden[:, at : at + wide] = xrecv[k, :, low:].astype(F32) + res_y[
            :, :, at : at + wide
        ].reshape(NY * 8, wide)
    held = hidden[...]
    squares[y] = jnp.broadcast_to(jnp.sum(held * held, axis=1, keepdims=True), (NY * 8, 128))
    for d in range(1, NY):
        send(squares.at[y], squares.at[y], sq_s.at[d], sq_r.at[d], y=wrap(y + d, NY))
    for d in range(1, NY):
        arrived(squares.at[wrap(y - d, NY)], sq_s.at[d], sq_r.at[d])
    for d in (1, 3, 2):
        send_weights(2, d)
    mean = (squares[0] + squares[1] + squares[2] + squares[3])[:, :1] * (1.0 / D)
    tokens[1] = (held * lax.rsqrt(mean + NORM_EPS) * gain[pl.ds(pl.multiple_of(y * DY, 256), DY)].astype(F32).reshape(1, DY)).astype(BF16)
    token_ring = ring_gather(
        links, "z", NZ, z,
        lambda k, shift: tokens.at[(1 - k + shift) % NZ],
        lambda ref, h: ref.at[pl.ds(h * 16, 16)],
        tk_s, tk_r,
    )

    def dispatch(h):
        table = tokens[4 * h : 4 * h + 4].reshape(128, DY)
        chosen = jnp.dot(choose[h], table, preferred_element_type=F32).astype(BF16)
        for k in range(NX):
            disp[h, k] = chosen[k * HALF : (k + 1) * HALF]
        for d in (2, 1, 3):
            to = wrap(x + d, NX)
            send(disp.at[h, to], rows.at[x, h], dp_s.at[h, d], dp_r.at[h, d], x=to)
        rows[x, h] = disp[h, x]

    next(token_ring)
    next(token_ring)
    dispatch(0)
    next(token_ring)
    for k in range(2):
        pass_on(k, 2)
    drain(token_ring)
    dispatch(1)
    for k in range(2):
        from_other(k)

    def enter(h):
        for d in range(1, NX):
            arrived(rows.at[wrap(x - d, NX), h], dp_s.at[h, d], dp_r.at[h, d])

        def inward(j, _):
            at = pl.ds(pl.multiple_of(j * 512, 512), 512)
            part = jnp.dot(
                rows[:, h].reshape(NX * HALF, DY), w_in[:, at], preferred_element_type=F32
            ).astype(BF16)
            for k in range(NX):
                gsend[k, h, :, at] = part[k * HALF : (k + 1) * HALF]
            return 0

        lax.fori_loop(0, 2 * FF // 512, inward, 0)

    def inward_term(h):
        return lambda k, part: gsend[
            wrap(y + k, NY), h, :, part * FF : (part + 1) * FF
        ].astype(F32)

    def sum_ring(h):
        return ring_reduce(
            links, "y", NY, y, inward_term(h), g_sent.at[h], g_got.at[h], gy_s.at[h], gy_r.at[h]
        )

    def activate(h):
        gate, up = (
            inward_term(h)(0, part)
            + g_got[h, 0, NY // 2, part].astype(F32)
            + g_got[h, 1, NY // 2, part].astype(F32)
            for part in range(2)
        )
        act[y, h] = (gate / (1.0 + jnp.exp(-gate)) * up).astype(BF16)

    def act_ring(h):
        return ring_gather(
            links, "y", NY, y, lambda k, shift: act.at[wrap(y + k, NY), h],
            lambda ref, part: ref.at[:, pl.ds(part * (FF // 2), FF // 2)],
            ac_s.at[h], ac_r.at[h],
        )

    def leave(h):
        def outward(j, _):
            at = pl.ds(pl.multiple_of(j * 256, 256), 256)
            part = jnp.dot(
                act[:, h].reshape(NX * HALF, FF), w_out[:, at], preferred_element_type=F32
            ).astype(BF16)
            for k in range(NX):
                dout[h, k, :, at] = part[k * HALF : (k + 1) * HALF]
            return 0

        lax.fori_loop(0, DY // 256, outward, 0)
        for d in (2, 1, 3):
            to = wrap(x + d, NX)
            send(dout.at[h, to], back.at[h, x], bk_s.at[h, d], bk_r.at[h, d], x=to)
        back[h, x] = dout[h, x]

    sums = [sum_ring(0), sum_ring(1)]
    acts = [act_ring(0), act_ring(1)]
    enter(0)
    for _ in range(3):
        next(sums[0])
    enter(1)
    next(sums[1])
    next(sums[1])
    drain(sums[0])
    activate(0)
    next(acts[0])
    next(acts[0])
    next(sums[1])
    drain(acts[0])
    for d in (1, 3, 2):
        pass_on(2, d)
    drain(sums[1])
    activate(1)
    next(acts[1])
    from_other(2)
    leave(0)
    drain(acts[1])
    leave(1)

    def weigh_rows(h):
        for d in range(1, NX):
            arrived(back.at[h, wrap(x - d, NX)], bk_s.at[h, d], bk_r.at[h, d])

        def gather(j, _):
            at = pl.ds(pl.multiple_of(j * 256, 256), 256)
            part = jnp.dot(
                combine[h], back[h, :, :, at].reshape(NX * HALF, 256), preferred_element_type=F32
            )
            for k in range(4):
                comb[4 * h + k, :, at] = part[k * 32 : (k + 1) * 32]
            return 0

        lax.fori_loop(0, DY // 256, gather, 0)

    def token_term(k, h):
        return comb[(1 - k) % NZ, h * 16 : (h + 1) * 16]

    weigh_rows(0)
    weigh_rows(1)
    drain(ring_reduce(links, "z", NZ, z, token_term, c_sent, c_got, zc_s, zc_r))
    for h in range(2):
        total = (
            hidden[h * 16 : (h + 1) * 16]
            + token_term(0, h)
            + c_got[0, NZ // 2, h].astype(F32)
            + c_got[1, NZ // 2, h].astype(F32)
        )
        for k in range(2):
            block = total[k * 8 : (k + 1) * 8]
            fin[2 * h + k] = jnp.concatenate(
                [block[:, : DY // 2], block[:, DY // 2 :]], axis=0
            ).astype(BF16)
    for d in (2, 1, 3):
        to = wrap(y + d, NY)
        send(fin.at[to], orecv.at[y], fo_s.at[d], fo_r.at[d], y=to)
    orecv[y] = fin[y]
    for d in range(1, NY):
        arrived(orecv.at[wrap(y - d, NY)], fo_s.at[d], fo_r.at[d])
    for k in range(NY):
        block = orecv[k].astype(F32)
        out[:, k * DY : k * DY + DY // 2] = block[:8]
        out[:, k * DY + DY // 2 : (k + 1) * DY] = block[8:]
    links.finish()


def layer(*operands):
    def two(*shape):
        return [DMA(shape), DMA(shape)]

    return pl.pallas_call(
        layer_kernel,
        out_shape=jax.ShapeDtypeStruct((8, D), F32),
        in_specs=[SMEM] + [ANY] * 12,
        out_specs=VMEM,
        scratch_shapes=[
            pltpu.VMEM((2, 256, LAT + ROPE), BF16),
            pltpu.VMEM((2, LAT + ROPE, 256), BF16),
            pltpu.VMEM((2, LAT, HD), BF16),
            pltpu.VMEM((8, TOP), F32),
            pltpu.VMEM((8, D), BF16),
            pltpu.VMEM((8, TOP), jnp.int32),
            pltpu.VMEM((4, ANC), jnp.int32),
            pltpu.VMEM((D,), BF16),
            pltpu.VMEM((32, BLK, LAT + ROPE), BF16),
            pltpu.VMEM(((ANC + 1) * BLK, LAT + ROPE), BF16),
            pltpu.VMEM((8, 128), F32),
            pltpu.VMEM((NZ, NY, 8, 128), F32),
            pltpu.VMEM((8, D), F32),
            pltpu.VMEM((NY, 8, DY), F32),
            pltpu.VMEM((NX, 256, CW), BF16),
            pltpu.VMEM((NY, NX, 128, 256), BF16),
            pltpu.VMEM((NX, NY, 128, 256), BF16),
            pltpu.VMEM((NZ, NY, 32, CW), BF16),
            pltpu.VMEM((2, NZ // 2 + 1, 2, 2, 32, CW), BF16),
            pltpu.VMEM((2, NZ // 2 + 1, 2, 2, 32, CW), BF16),
            pltpu.VMEM((NX, NY * 8, CW), BF16),
            pltpu.VMEM((NX, NY * 8, CW), BF16),
            pltpu.VMEM((NY * 8, DY), F32),
            pltpu.VMEM((NY, NY * 8, 128), F32),
            pltpu.VMEM((NZ, NY * 8, DY), BF16),
            pltpu.VMEM((2, NX * HALF, 128), BF16),
            pltpu.VMEM((2, 128, NX * HALF), BF16),
            pltpu.VMEM((2, NX, HALF, DY), BF16),
            pltpu.VMEM((NX, 2, HALF, DY), BF16),
            pltpu.VMEM((DY, 2 * FF), BF16),
            pltpu.VMEM((FF, DY), BF16),
            pltpu.VMEM((NY, 2, HALF, 2 * FF), BF16),
            pltpu.VMEM((2, 2, NY // 2 + 1, 2, HALF, FF), BF16),
            pltpu.VMEM((2, 2, NY // 2 + 1, 2, HALF, FF), BF16),
            pltpu.VMEM((NY, 2, HALF, FF), BF16),
            pltpu.VMEM((2, NX, HALF, DY), BF16),
            pltpu.VMEM((2, NX, HALF, DY), BF16),
            pltpu.VMEM((NZ, NY * 8, DY), F32),
            pltpu.VMEM((2, NZ // 2 + 1, 2, 16, DY), BF16),
            pltpu.VMEM((2, NZ // 2 + 1, 2, 16, DY), BF16),
            pltpu.VMEM((NY, 16, DY // 2), BF16),
            pltpu.VMEM((NY, 16, DY // 2), BF16),
            DMA((12,)),
            *two(2, NY // 2 + 1, 2),
            *two(NY),
            *two(NX),
            *two(NY),
            *two(NZ),
            *two(NY),
            *two(NX),
            *two(NY),
            *two(2, NY // 2 + 1, 2),
            *two(2, NX // 2 + 1, 2),
            *two(2, NZ // 2 + 1, 2),
            *two(NX),
            *two(NY),
            *two(2, NZ // 2 + 1, 2),
            *two(2, NX),
            *two(3, NY),
            *two(3, NY),
            *two(2, 2, NY // 2 + 1, 2),
            *two(2, 2, NY // 2 + 1, 2),
            *two(2, NX),
            *two(2, NZ // 2 + 1, 2),
            *two(NY),
        ],
        compiler_params=pltpu.CompilerParams(
            collective_id=0, has_side_effects=True, vmem_limit_bytes=63 << 20
        ),
        name="layer",
    )(*operands)


def on_device(
    queries,
    latent_cache,
    ancestors,
    value_up,
    out_proj,
    residual,
    norm_gain,
    routes,
    gates,
    w_gate,
    w_up,
    w_down,
):
    final = layer(
        ancestors,
        queries.transpose(1, 2, 0),
        value_up,
        gates,
        residual,
        routes,
        ancestors,
        norm_gain,
        latent_cache,
        out_proj,
        w_gate[0],
        w_up[0],
        w_down[0],
    )
    return final.astype(BF16)


def solution(mesh):
    placed = (
        P("seq", "exp", None),
        P("seq", None, None),
        P("seq", None),
        P("exp", None, None),
        P("exp", None),
        P(("seq", "exp"), None),
        P(),
        P(("seq", "exp"), None),
        P(("seq", "exp"), None),
        P("exp", None, "seq"),
        P("exp", None, "seq"),
        P("exp", "seq", None),
    )
    return jax.shard_map(
        on_device, mesh=mesh, in_specs=placed, out_specs=P(("seq", "exp"), None), check_vma=False
    )
```

```python
import jax
import jax.numpy as jnp
from jax import lax
from jax.experimental import pallas as pl
from jax.experimental.pallas import tpu as pltpu
from jax.sharding import PartitionSpec as P

D = 7168
LAT = 512
ROPE = 64
HD = 128
BLK = 64
ANC = 8
TOP = 8
CAP = 3
NY, NZ, NX = 4, 8, 4
DY = D // NY
CW = 512
FF = 1024
HALF = 48
UNNAMED = 99.0
NORM_EPS = 1e-6
MASKED = -1e30
F32 = jnp.float32
BF16 = jnp.bfloat16
ANY = pl.BlockSpec(memory_space=pl.ANY)
VMEM = pl.BlockSpec(memory_space=pltpu.VMEM)
SMEM = pl.BlockSpec(memory_space=pltpu.SMEM)
DMA = pltpu.SemaphoreType.DMA


def place():
    s = lax.axis_index("seq")
    e = lax.axis_index("exp")
    return lax.div(s, 2), lax.rem(s, 2), lax.div(e, NX), lax.rem(e, NX)


def wrap(value, count):
    return lax.rem(value + count, count)


def meet(peers):
    barrier = pltpu.get_barrier_semaphore()
    for y, c, z, x in peers:
        pl.semaphore_signal(
            barrier,
            inc=1,
            device_id=(y * 2 + c, z * NX + x),
            device_id_type=pl.DeviceIdType.MESH,
        )
    pl.semaphore_wait(barrier, len(peers))


class Links:
    def __init__(self, y, c, z, x):
        self.at = (y, c, z, x)
        self.started = []

    def copy(self, src, dst, send_sem, recv_sem, y=None, c=None, z=None, x=None):
        here = self.at
        y, c, z, x = (own if new is None else new for new, own in zip((y, c, z, x), here))
        return pltpu.make_async_remote_copy(
            src_ref=src,
            dst_ref=dst,
            send_sem=send_sem,
            recv_sem=recv_sem,
            device_id=(y * 2 + c, z * NX + x),
            device_id_type=pl.DeviceIdType.MESH,
        )

    def send(self, src, dst, send_sem, recv_sem, **to):
        copy = self.copy(src, dst, send_sem, recv_sem, **to)
        copy.start()
        self.started.append(copy)

    def arrived(self, dst, send_sem, recv_sem):
        self.copy(dst, dst, send_sem, recv_sem).wait_recv()

    def finish(self):
        for copy in self.started:
            copy.wait_send()


def ring_gather(links, axis, count, me, view, half, send_sem, recv_sem):
    last = count // 2

    def got(way, step, part):
        links.arrived(
            half(view(-(1, -1)[way] * step, 0), part),
            send_sem.at[way, step, part],
            recv_sem.at[way, step, part],
        )

    for step in range(1, last + 1):
        new = []
        for part_at in range(2):
            for way, sign in enumerate((1, -1)):
                part = way if part_at == 0 else 1 - way
                k = -sign * (step - 1)
                if step > 1:
                    got(way, step - 1, part)
                    if part_at:
                        new.append(k)
                if step < last or part == way:
                    links.send(
                        half(view(k, 0), part), half(view(k, sign), part),
                        send_sem.at[way, step, part], recv_sem.at[way, step, part],
                        **{axis: wrap(me + sign, count)},
                    )
        if new:
            yield new
    for way in range(2):
        got(way, last, way)
    yield [last]


def ring_reduce(links, axis, count, me, own, sent, got, send_sem, recv_sem):
    last = count // 2
    for step in range(1, last + 1):
        yield step
        for part_at in range(2):
            for way, sign in enumerate((1, -1)):
                h = 1 - way if part_at == 0 else way
                if step == 1 and h != way:
                    continue
                value = own(sign * (last + 1 - step), h)
                if step > 2 or (step == 2 and h == way):
                    links.arrived(
                        got.at[way, step - 1, h],
                        send_sem.at[way, step - 1, h],
                        recv_sem.at[way, step - 1, h],
                    )
                    value = value + got[way, step - 1, h].astype(F32)
                sent[way, step, h] = value.astype(BF16)
                links.send(
                    sent.at[way, step, h], got.at[way, step, h],
                    send_sem.at[way, step, h], recv_sem.at[way, step, h],
                    **{axis: wrap(me + sign, count)},
                )
    yield last + 1
    for h in range(2):
        for way in range(2):
            links.arrived(
                got.at[way, last, h], send_sem.at[way, last, h], recv_sem.at[way, last, h]
            )


def drain(steps):
    for _ in steps:
        pass


def routing_table(routes, gates):
    lane = lax.broadcasted_iota(jnp.int32, (8, 128), 1)
    gate = jnp.zeros((8, 128), F32)
    named = jnp.zeros((8, 128), F32)
    for k in range(TOP):
        expert = routes[:, k : k + 1]
        gate = gate + jnp.where(expert == lane, gates[:, k : k + 1], 0.0)
        named = named + jnp.where(expert == lane - 32, 1.0, 0.0)
    row = lax.broadcasted_iota(jnp.int32, (8, 8), 0)
    col = lax.broadcasted_iota(jnp.int32, (8, 8), 1)
    before = jnp.dot((col < row).astype(F32), named, preferred_element_type=F32)
    return jnp.where(lane < 32, gate, jnp.where(named > 0.5, before, UNNAMED))


def matches(table, z):
    lane = lax.broadcasted_iota(jnp.int32, (128, 128), 1)
    row = lax.broadcasted_iota(jnp.int32, (128, NX * HALF), 1)
    token = lax.broadcasted_iota(jnp.int32, (128, NX * HALF), 0)
    slot = jnp.zeros((128, NX * HALF), F32)
    gate = jnp.zeros((128, NX * HALF), F32)
    for k in range(NX):
        expert = z * NX + k
        gate_col = jnp.sum(jnp.where(lane == expert, table, 0.0), axis=1, keepdims=True)
        slot_col = jnp.sum(jnp.where(lane == expert + 32, table, 0.0), axis=1, keepdims=True)
        mine = jnp.logical_and(row >= k * HALF, row < (k + 1) * HALF)
        slot = jnp.where(mine, slot_col, slot)
        gate = jnp.where(mine, gate_col, gate)
    inner = lax.rem(row, HALF)
    hit = jnp.logical_and(
        lax.div(token, 8) == lax.div(inner, CAP), slot == lax.rem(inner, CAP).astype(F32)
    )
    return jnp.where(hit, 1.0, 0.0).astype(BF16), jnp.where(hit, gate, 0.0).astype(BF16)


def attend(g, s, anc, live, q, lat, vup, keys):
    width = (ANC + 1) * BLK
    col = lax.broadcasted_iota(jnp.int32, (2 * BLK, width), 1)
    row = lax.rem(lax.broadcasted_iota(jnp.int32, (2 * BLK, width), 0), BLK)
    for a in range(ANC):
        keys[a * BLK : (a + 1) * BLK, :] = lat[jnp.maximum(anc[g, a], 0)]
    keys[ANC * BLK :, :] = lat[s * 4 + g]
    query = q[:, g * BLK : (g + 1) * BLK, :].reshape(2 * BLK, LAT + ROPE)
    scores = lax.dot_general(
        query, keys[...], (((1,), (1,)), ((), ())), preferred_element_type=F32
    ) * ((HD + ROPE) ** (-0.5))
    mask = jnp.logical_and(row >= col - ANC * BLK, live[g : g + 1, :] > 0.5)
    highest = jnp.max(jnp.where(mask, scores, MASKED), axis=1, keepdims=True)
    weights = jnp.where(mask, jnp.exp(scores - highest), 0.0)
    total = jnp.sum(weights, axis=1, keepdims=True)
    summed = jnp.dot(weights.astype(BF16), keys[:, :LAT], preferred_element_type=F32)
    latent = (summed / total).astype(BF16)
    return jnp.concatenate(
        [
            jnp.dot(latent[h * BLK : (h + 1) * BLK], vup[h], preferred_element_type=F32)
            for h in range(2)
        ],
        axis=1,
    ).astype(BF16)


def layer_kernel(
    anc, q_in, vup_in, gates_in, res_in, routes_in, anc_in, gain_in, lat_in, outp, wg, wu, wd,
    out,
    q, q_turned, vup, gates, res, routes, anc_rows, gain,
    lat, keys, meta, meta_all, res32, res_y, op_all, ho_a, ho_b, partial, a_sent, a_got,
    att, xrecv, hidden, squares, tokens, choose, combine, disp, rows, w_in, w_out,
    gsend, g_sent, g_got, act, dout, back, comb, c_sent, c_got, fin, orecv,
    loc, lat_s, lat_r, fwd_s, fwd_r, op_s, op_r, me_s, me_r, mz_s, mz_r, re_s, re_r,
    a1_s, a1_r, b1_s, b1_r, a2_s, a2_r, b2_s, b2_r, za_s, za_r, xa_s, xa_r, sq_s, sq_r,
    tk_s, tk_r, dp_s, dp_r, w_s, w_r, f_s, f_r, gy_s, gy_r, ac_s, ac_r, bk_s, bk_r,
    zc_s, zc_r, fo_s, fo_r,
):
    y, c, z, x = place()
    s = y * 2 + c
    other = 1 - c
    links = Links(y, c, z, x)
    send, arrived = links.send, links.arrived

    def weight_source(k, to):
        at = pl.ds(pl.multiple_of(to * DY, 128), DY)
        return (wg.at[at, :], wu.at[at, :], wd.at[:, at])[k]

    def weight_place(k, src):
        if k == 2:
            return w_out.at[pl.ds(pl.multiple_of(src * 128, 128), 128), :]
        return w_in.at[:, pl.ds(pl.multiple_of(k * FF + src * 128, 128), 128)]

    def send_weights(k, d):
        to = wrap(y + d, NY)
        send(weight_source(k, to), weight_place(k, s), w_s.at[k, d], w_r.at[k, d], y=to)

    def pass_on(k, d):
        block = weight_place(k, wrap(y - d, NY) * 2 + c)
        arrived(block, w_s.at[k, d], w_r.at[k, d])
        send(block, block, f_s.at[k, d], f_r.at[k, d], c=other)

    def from_other(k):
        own[2 + k].wait()
        for d in range(NY):
            block = weight_place(k, wrap(y - d, NY) * 2 + other)
            arrived(block, f_s.at[k, d], f_r.at[k, d])

    def op_columns(to):
        start = pl.multiple_of(y * DY + jnp.minimum(to * CW, DY - CW), 128)
        return outp.at[:, pl.ds(start, CW)]

    own = [
        pltpu.make_async_copy(lat_in, lat.at[pl.ds(s * 4, 4)], loc.at[0]),
        pltpu.make_async_copy(op_columns(x), op_all.at[x], loc.at[1]),
    ] + [
        pltpu.make_async_copy(weight_source(k, y), weight_place(k, s), loc.at[2 + k])
        for k in range(3)
    ]
    small = [
        pltpu.make_async_copy(src, dst, loc.at[5 + k])
        for k, (src, dst) in enumerate(
            (
                (routes_in, routes),
                (gates_in, gates),
                (res_in, res),
                (anc_in, anc_rows),
                (gain_in, gain),
                (q_in, q_turned),
                (vup_in, vup),
            )
        )
    ]
    for copy in own[:1] + small + own[1:]:
        copy.start()
    for copy in small[:3]:
        copy.wait()
    meta[...] = routing_table(routes[...], gates[...])
    meta_all[1, y] = meta[...]
    res32[...] = res[...].astype(F32)
    meet(
        [(wrap(y + d, NY), c, z, x) for d in range(1, NY)]
        + [(y, c, wrap(z + d, NZ), x) for d in range(1, NZ)]
        + [(y, c, z, wrap(x + d, NX)) for d in range(1, NX)]
        + [(y, other, z, x)]
    )

    own[0].wait()

    def lat_view(k, shift):
        return lat.at[pl.ds((wrap(y + k, NY) * 2 + c) * 4, 4)]

    lat_ring = ring_gather(
        links, "y", NY, y, lat_view, lambda ref, h: ref.at[pl.ds(h * 2, 2)], lat_s, lat_r
    )

    def forward(k):
        block = lat_view(k, 0)
        send(block, block, fwd_s.at[k % NY], fwd_r.at[k % NY], c=other)

    for d in range(1, NY):
        to = wrap(y + d, NY)
        send(meta, meta_all.at[1, y], me_s.at[d], me_r.at[d], y=to)
    first = next(lat_ring)
    forward(0)
    for k in first:
        forward(k)
    for k in range(2):
        for d in (1, 3):
            send_weights(k, d)
    for d in range(1, NX):
        to = wrap(x + d, NX)
        send(op_columns(to), op_all.at[x], op_s.at[d], op_r.at[d], x=to)
    for d in range(1, NY):
        arrived(meta_all.at[1, wrap(y - d, NY)], me_s.at[d], me_r.at[d])
    for d in range(1, NZ):
        send(meta_all.at[1], meta_all.at[(d + 1) % NZ], mz_s.at[d], mz_r.at[d], z=wrap(z + d, NZ))
    res_y[y] = res32[:, pl.ds(pl.multiple_of(y * DY, 128), DY)]
    for copy in small[3:]:
        copy.wait()
    for h in range(2):
        q[h] = q_turned[h].T
    area = lax.broadcasted_iota(jnp.int32, (ANC, (ANC + 1) * BLK), 1)
    slot_of = lax.broadcasted_iota(jnp.int32, (ANC, (ANC + 1) * BLK), 0)
    spread = (lax.div(area, BLK) == slot_of).astype(F32)
    live = jnp.dot((anc_rows[...] >= 0).astype(F32), spread, preferred_element_type=F32) + (
        lax.broadcasted_iota(jnp.int32, (4, (ANC + 1) * BLK), 1) >= ANC * BLK
    ).astype(F32)
    for new in lat_ring:
        for k in new:
            forward(k)
    for k in range(3):
        send(
            weight_source(k, y), weight_place(k, s), f_s.at[k, 0], f_r.at[k, 0], c=other
        )
    for k in range(NY):
        block = lat.at[pl.ds((wrap(y + k, NY) * 2 + other) * 4, 4)]
        arrived(block, fwd_s.at[k], fwd_r.at[k])

    for g in range(2):
        ho_a[y, x, g * BLK : (g + 1) * BLK, :] = attend(g, s, anc, live, q, lat, vup, keys)
    for d in range(1, NX):
        send(ho_a.at[y, x], ho_a.at[y, x], a1_s.at[d], a1_r.at[d], x=wrap(x + d, NX))
    for g in range(2):
        ho_b[x, y, g * BLK : (g + 1) * BLK, :] = attend(g + 2, s, anc, live, q, lat, vup, keys)
    for d in range(1, NY):
        send(ho_b.at[x, y], ho_b.at[x, y], b1_s.at[d], b1_r.at[d], y=wrap(y + d, NY))

    def pairs(ref, h):
        return ref.at[pl.ds(h * 2, 2)]

    a_ring = ring_gather(
        links, "y", NY, y, lambda k, shift: ho_a.at[wrap(y + k, NY)], pairs, a2_s, a2_r
    )
    b_ring = ring_gather(
        links, "x", NX, x, lambda k, shift: ho_b.at[wrap(x + k, NX)], pairs, b2_s, b2_r
    )
    for d in range(1, NX):
        arrived(ho_a.at[y, wrap(x - d, NX)], a1_s.at[d], a1_r.at[d])
    for d in range(1, NY):
        arrived(ho_b.at[x, wrap(y - d, NY)], b1_s.at[d], b1_r.at[d])
    next(a_ring)
    next(b_ring)
    for d in range(1, NZ):
        arrived(meta_all.at[(d + 1) % NZ], mz_s.at[d], mz_r.at[d])
    for h in range(2):
        pick, weigh = matches(meta_all[4 * h : 4 * h + 4].reshape(128, 128), z)
        choose[h] = pick.T
        combine[h] = weigh
    for d in range(1, NX):
        arrived(op_all.at[wrap(x - d, NX)], op_s.at[d], op_r.at[d])
    own[1].wait()
    drain(a_ring)
    drain(b_ring)
    for d in range(1, NY):
        to = wrap(y + d, NY)
        part = res32.at[:, pl.ds(pl.multiple_of(to * DY, 128), DY)]
        send(part, res_y.at[y], re_s.at[d], re_r.at[d], y=to)
    send_weights(0, 2)
    send_weights(1, 2)
    for k in range(2):
        for d in (1, 3):
            pass_on(k, d)

    for n in range(NY):
        for low, block in ((0, lambda k: ho_a[n, k]), (4, lambda k: ho_b[k, n])):
            total = None
            for k in range(NX):
                part = jnp.dot(block(k), op_all[k], preferred_element_type=F32)
                total = part if total is None else total + part
            total = total.astype(BF16)
            for k in range(4):
                partial[low + k, n] = total[k * 32 : (k + 1) * 32]

    def attention_term(k, h):
        return partial[wrap(z + k, NZ), 2 * h : 2 * h + 2].astype(F32)

    drain(ring_reduce(links, "z", NZ, z, attention_term, a_sent, a_got, za_s, za_r))
    summed = jnp.concatenate(
        [
            attention_term(0, h)
            + a_got[0, NZ // 2, h].astype(F32)
            + a_got[1, NZ // 2, h].astype(F32)
            for h in range(2)
        ],
        axis=0,
    )
    for k in range(NX):
        att[k] = summed[:, k * 8 : (k + 1) * 8].reshape(NY * 8, CW).astype(BF16)
    for d in range(1, NX):
        to = wrap(x + d, NX)
        send(att.at[to], xrecv.at[x], xa_s.at[d], xa_r.at[d], x=to)
    xrecv[x] = att[x]
    for d in range(1, NY):
        arrived(res_y.at[wrap(y - d, NY)], re_s.at[d], re_r.at[d])
    for d in range(1, NX):
        arrived(xrecv.at[wrap(x - d, NX)], xa_s.at[d], xa_r.at[d])
    for k in range(NX):
        low = NX * CW - DY if k == NX - 1 else 0
        at, wide = k * CW, CW - low
        hidden[:, at : at + wide] = xrecv[k, :, low:].astype(F32) + res_y[
            :, :, at : at + wide
        ].reshape(NY * 8, wide)
    held = hidden[...]
    squares[y] = jnp.broadcast_to(jnp.sum(held * held, axis=1, keepdims=True), (NY * 8, 128))
    for d in range(1, NY):
        send(squares.at[y], squares.at[y], sq_s.at[d], sq_r.at[d], y=wrap(y + d, NY))
    for d in range(1, NY):
        arrived(squares.at[wrap(y - d, NY)], sq_s.at[d], sq_r.at[d])
    for d in (1, 3):
        send_weights(2, d)
    mean = (squares[0] + squares[1] + squares[2] + squares[3])[:, :1] * (1.0 / D)
    tokens[1] = (held * lax.rsqrt(mean + NORM_EPS) * gain[pl.ds(pl.multiple_of(y * DY, 256), DY)].astype(F32).reshape(1, DY)).astype(BF16)
    token_ring = ring_gather(
        links, "z", NZ, z,
        lambda k, shift: tokens.at[(1 - k + shift) % NZ],
        lambda ref, h: ref.at[pl.ds(h * 16, 16)],
        tk_s, tk_r,
    )

    def dispatch(h):
        table = tokens[4 * h : 4 * h + 4].reshape(128, DY)
        chosen = jnp.dot(choose[h], table, preferred_element_type=F32).astype(BF16)
        for k in range(NX):
            disp[h, k] = chosen[k * HALF : (k + 1) * HALF]
        for d in (2, 1, 3):
            to = wrap(x + d, NX)
            send(disp.at[h, to], rows.at[x, h], dp_s.at[h, d], dp_r.at[h, d], x=to)
        rows[x, h] = disp[h, x]

    next(token_ring)
    next(token_ring)
    dispatch(0)
    next(token_ring)
    for k in range(2):
        pass_on(k, 2)
    drain(token_ring)
    dispatch(1)
    for k in range(2):
        from_other(k)

    def enter(h):
        for d in range(1, NX):
            arrived(rows.at[wrap(x - d, NX), h], dp_s.at[h, d], dp_r.at[h, d])

        def inward(j, _):
            at = pl.ds(pl.multiple_of(j * 512, 512), 512)
            part = jnp.dot(
                rows[:, h].reshape(NX * HALF, DY), w_in[:, at], preferred_element_type=F32
            ).astype(BF16)
            for k in range(NX):
                gsend[k, h, :, at] = part[k * HALF : (k + 1) * HALF]
            return 0

        lax.fori_loop(0, 2 * FF // 512, inward, 0)

    def inward_term(h):
        return lambda k, part: gsend[
            wrap(y + k, NY), h, :, part * FF : (part + 1) * FF
        ].astype(F32)

    def sum_ring(h):
        return ring_reduce(
            links, "y", NY, y, inward_term(h), g_sent.at[h], g_got.at[h], gy_s.at[h], gy_r.at[h]
        )

    def activate(h):
        gate, up = (
            inward_term(h)(0, part)
            + g_got[h, 0, NY // 2, part].astype(F32)
            + g_got[h, 1, NY // 2, part].astype(F32)
            for part in range(2)
        )
        act[y, h] = (gate / (1.0 + jnp.exp(-gate)) * up).astype(BF16)

    def act_ring(h):
        return ring_gather(
            links, "y", NY, y, lambda k, shift: act.at[wrap(y + k, NY), h],
            lambda ref, part: ref.at[:, pl.ds(part * (FF // 2), FF // 2)],
            ac_s.at[h], ac_r.at[h],
        )

    def leave(h):
        def outward(j, _):
            at = pl.ds(pl.multiple_of(j * 256, 256), 256)
            part = jnp.dot(
                act[:, h].reshape(NX * HALF, FF), w_out[:, at], preferred_element_type=F32
            ).astype(BF16)
            for k in range(NX):
                dout[h, k, :, at] = part[k * HALF : (k + 1) * HALF]
            return 0

        lax.fori_loop(0, DY // 256, outward, 0)
        for d in (2, 1, 3):
            to = wrap(x + d, NX)
            send(dout.at[h, to], back.at[h, x], bk_s.at[h, d], bk_r.at[h, d], x=to)
        back[h, x] = dout[h, x]

    sums = [sum_ring(0), sum_ring(1)]
    acts = [act_ring(0), act_ring(1)]
    enter(0)
    for _ in range(3):
        next(sums[0])
    send_weights(2, 2)
    enter(1)
    next(sums[1])
    next(sums[1])
    drain(sums[0])
    activate(0)
    next(acts[0])
    next(acts[0])
    next(sums[1])
    drain(acts[0])
    for d in (1, 3, 2):
        pass_on(2, d)
    drain(sums[1])
    activate(1)
    next(acts[1])
    from_other(2)
    leave(0)
    drain(acts[1])
    leave(1)

    def weigh_rows(h):
        for d in range(1, NX):
            arrived(back.at[h, wrap(x - d, NX)], bk_s.at[h, d], bk_r.at[h, d])

        def gather(j, _):
            at = pl.ds(pl.multiple_of(j * 256, 256), 256)
            part = jnp.dot(
                combine[h], back[h, :, :, at].reshape(NX * HALF, 256), preferred_element_type=F32
            )
            for k in range(4):
                comb[4 * h + k, :, at] = part[k * 32 : (k + 1) * 32]
            return 0

        lax.fori_loop(0, DY // 256, gather, 0)

    def token_term(k, h):
        return comb[(1 - k) % NZ, h * 16 : (h + 1) * 16]

    weigh_rows(0)
    weigh_rows(1)
    drain(ring_reduce(links, "z", NZ, z, token_term, c_sent, c_got, zc_s, zc_r))
    for h in range(2):
        total = (
            hidden[h * 16 : (h + 1) * 16]
            + token_term(0, h)
            + c_got[0, NZ // 2, h].astype(F32)
            + c_got[1, NZ // 2, h].astype(F32)
        )
        for k in range(2):
            block = total[k * 8 : (k + 1) * 8]
            fin[2 * h + k] = jnp.concatenate(
                [block[:, : DY // 2], block[:, DY // 2 :]], axis=0
            ).astype(BF16)
    for d in (2, 1, 3):
        to = wrap(y + d, NY)
        send(fin.at[to], orecv.at[y], fo_s.at[d], fo_r.at[d], y=to)
    orecv[y] = fin[y]
    for d in range(1, NY):
        arrived(orecv.at[wrap(y - d, NY)], fo_s.at[d], fo_r.at[d])
    for k in range(NY):
        block = orecv[k].astype(F32)
        out[:, k * DY : k * DY + DY // 2] = block[:8]
        out[:, k * DY + DY // 2 : (k + 1) * DY] = block[8:]
    links.finish()


def layer(*operands):
    def two(*shape):
        return [DMA(shape), DMA(shape)]

    return pl.pallas_call(
        layer_kernel,
        out_shape=jax.ShapeDtypeStruct((8, D), F32),
        in_specs=[SMEM] + [ANY] * 12,
        out_specs=VMEM,
        scratch_shapes=[
            pltpu.VMEM((2, 256, LAT + ROPE), BF16),
            pltpu.VMEM((2, LAT + ROPE, 256), BF16),
            pltpu.VMEM((2, LAT, HD), BF16),
            pltpu.VMEM((8, TOP), F32),
            pltpu.VMEM((8, D), BF16),
            pltpu.VMEM((8, TOP), jnp.int32),
            pltpu.VMEM((4, ANC), jnp.int32),
            pltpu.VMEM((D,), BF16),
            pltpu.VMEM((32, BLK, LAT + ROPE), BF16),
            pltpu.VMEM(((ANC + 1) * BLK, LAT + ROPE), BF16),
            pltpu.VMEM((8, 128), F32),
            pltpu.VMEM((NZ, NY, 8, 128), F32),
            pltpu.VMEM((8, D), F32),
            pltpu.VMEM((NY, 8, DY), F32),
            pltpu.VMEM((NX, 256, CW), BF16),
            pltpu.VMEM((NY, NX, 128, 256), BF16),
            pltpu.VMEM((NX, NY, 128, 256), BF16),
            pltpu.VMEM((NZ, NY, 32, CW), BF16),
            pltpu.VMEM((2, NZ // 2 + 1, 2, 2, 32, CW), BF16),
            pltpu.VMEM((2, NZ // 2 + 1, 2, 2, 32, CW), BF16),
            pltpu.VMEM((NX, NY * 8, CW), BF16),
            pltpu.VMEM((NX, NY * 8, CW), BF16),
            pltpu.VMEM((NY * 8, DY), F32),
            pltpu.VMEM((NY, NY * 8, 128), F32),
            pltpu.VMEM((NZ, NY * 8, DY), BF16),
            pltpu.VMEM((2, NX * HALF, 128), BF16),
            pltpu.VMEM((2, 128, NX * HALF), BF16),
            pltpu.VMEM((2, NX, HALF, DY), BF16),
            pltpu.VMEM((NX, 2, HALF, DY), BF16),
            pltpu.VMEM((DY, 2 * FF), BF16),
            pltpu.VMEM((FF, DY), BF16),
            pltpu.VMEM((NY, 2, HALF, 2 * FF), BF16),
            pltpu.VMEM((2, 2, NY // 2 + 1, 2, HALF, FF), BF16),
            pltpu.VMEM((2, 2, NY // 2 + 1, 2, HALF, FF), BF16),
            pltpu.VMEM((NY, 2, HALF, FF), BF16),
            pltpu.VMEM((2, NX, HALF, DY), BF16),
            pltpu.VMEM((2, NX, HALF, DY), BF16),
            pltpu.VMEM((NZ, NY * 8, DY), F32),
            pltpu.VMEM((2, NZ // 2 + 1, 2, 16, DY), BF16),
            pltpu.VMEM((2, NZ // 2 + 1, 2, 16, DY), BF16),
            pltpu.VMEM((NY, 16, DY // 2), BF16),
            pltpu.VMEM((NY, 16, DY // 2), BF16),
            DMA((12,)),
            *two(2, NY // 2 + 1, 2),
            *two(NY),
            *two(NX),
            *two(NY),
            *two(NZ),
            *two(NY),
            *two(NX),
            *two(NY),
            *two(2, NY // 2 + 1, 2),
            *two(2, NX // 2 + 1, 2),
            *two(2, NZ // 2 + 1, 2),
            *two(NX),
            *two(NY),
            *two(2, NZ // 2 + 1, 2),
            *two(2, NX),
            *two(3, NY),
            *two(3, NY),
            *two(2, 2, NY // 2 + 1, 2),
            *two(2, 2, NY // 2 + 1, 2),
            *two(2, NX),
            *two(2, NZ // 2 + 1, 2),
            *two(NY),
        ],
        compiler_params=pltpu.CompilerParams(
            collective_id=0, has_side_effects=True, vmem_limit_bytes=63 << 20
        ),
        name="layer",
    )(*operands)


def on_device(
    queries,
    latent_cache,
    ancestors,
    value_up,
    out_proj,
    residual,
    norm_gain,
    routes,
    gates,
    w_gate,
    w_up,
    w_down,
):
    final = layer(
        ancestors,
        queries.transpose(1, 2, 0),
        value_up,
        gates,
        residual,
        routes,
        ancestors,
        norm_gain,
        latent_cache,
        out_proj,
        w_gate[0],
        w_up[0],
        w_down[0],
    )
    return final.astype(BF16)


def solution(mesh):
    placed = (
        P("seq", "exp", None),
        P("seq", None, None),
        P("seq", None),
        P("exp", None, None),
        P("exp", None),
        P(("seq", "exp"), None),
        P(),
        P(("seq", "exp"), None),
        P(("seq", "exp"), None),
        P("exp", None, "seq"),
        P("exp", None, "seq"),
        P("exp", "seq", None),
    )
    return jax.shard_map(
        on_device, mesh=mesh, in_specs=placed, out_specs=P(("seq", "exp"), None), check_vma=False
    )
```
